128 devices in a mesh: dp: 8 (over y, x_lo), chan: 16 (over x_hi, z, core).
Axes of the slice: x: 4 (x_hi: 2, x_lo: 2; x = x_hi * 2 + x_lo), y: 4, z: 4, core: 2. Of those that a mesh axis runs over, the one named last changes fastest.
Arguments:
- tokens: int32 [2, 128], P(None, 'dp'), may hold values from 0 to 511
- parents: int32 [2, 128], replicated, may hold values from 0 to 127, as said below
- embed_table: bfloat16 [512, 8192], P(None, 'chan'), may hold values from -5 to 5
- norm_gain: float32 [2, 8192], P(None, 'chan'), may hold values from 0.1 to 1.9
- weight_in: bfloat16 [2, 16, 8, 3, 64, 8192], P(None, None, 'dp', None, None, 'chan'), may hold values from -0.0625 to 0.0625
- weight_out: bfloat16 [2, 16, 8, 64, 8192], P(None, None, 'dp', None, 'chan'), may hold values from -0.0625 to 0.0625
- fir_filters: float32 [512, 128], P('chan'), may hold values from -0.6 to 0.6
- mode_poles: float32 [16, 8192], P(None, 'chan'), may hold values from 0.3 to 0.99
- residues: float32 [16, 8192], P(None, 'chan'), may hold values from -1.5 to 1.5
- fir_cache: bfloat16 [128, 127, 8192], P('dp', None, 'chan'), may hold values from -6 to 6
- modal_state: float32 [128, 16, 8192], P('dp', None, 'chan'), may hold values from -12 to 12
Outputs:
- hidden_out: bfloat16 [2, 128, 8192], P(None, 'dp', 'chan')
- fir_next: bfloat16 [128, 127, 8192], P('dp', None, 'chan')
- state_next: float32 [128, 16, 8192], P('dp', None, 'chan')
The draws below stay inside these ranges and needn't reach their ends.
Inputs may be any that keep to these rules, and one draw needn't show every extreme that they name: `parents`: beams 2 * 16 * q to 2 * 16 * q + 2 * 16 - 1 form request q; at every step each beam's parent is a beam of its own request.
All inputs are finite; a program needn't handle non-finite values.
Results may differ from the reference program's by a relative error of at most 0.02.
Values may be sent and summed in bfloat16 or wider, within the bound.
No kernel may reach another device: no remote copies, remote signals or barrier semaphores. Data moves between devices by JAX's collectives and lax.ppermute only.
A program may use at most 128 MiB of HBM per device.

```python
import math
import jax
import jax.numpy as jnp
from jax import lax

D = 8192
VOCAB = 512
TAPS = 128
GROUP = 16
MODES = 16
STEPS = 2
BEAM_DEV = 16
BEAMS = 128
GROUPS = 512
PIECE = 64
N_DP = 8
N_CHAN = 16


def draw_parents(key, part):
    request = 2 * BEAM_DEV
    offsets = jax.random.randint(key, (STEPS, BEAMS), 0, request, dtype=jnp.int32)
    position = jnp.arange(BEAMS, dtype=jnp.int32) % request
    offsets = jnp.where(position[None, :] == 0, request - 1, offsets)
    offsets = jnp.where(position[None, :] == BEAM_DEV, 0, offsets)
    beam_ids = jnp.arange(BEAMS, dtype=jnp.int32)
    return (beam_ids[None, :] - position[None, :] + offsets).astype(jnp.int32)


def draw_embed_table(key, part):
    key_base, key_cols = jax.random.split(key, 2)
    column = jnp.arange(D, dtype=jnp.float32) / D
    roughness = jnp.exp(jax.random.uniform(key_cols, (D,), minval=0.0, maxval=math.log(10.0)))
    base_values = jnp.clip(jax.random.normal(key_base, (VOCAB, D)), -4.0, 4.0)
    trend_line = 1.0 + 2.0 * column
    scaled = 0.04 * base_values * roughness[None, :] * trend_line[None, :]
    return scaled.astype(jnp.bfloat16)


def plant(result, stream_key, low, high):
    spot = [jax.random.randint(jax.random.fold_in(stream_key, axis), (), 0, length) for axis, length in enumerate(result.shape)]
    widest = result.shape.index(max(result.shape))
    neighbour = spot[:widest] + [(spot[widest] + 1) % result.shape[widest]] + spot[widest + 1:]
    return result.at[tuple(spot)].set(low).at[tuple(neighbour)].set(high)


def level_of(key, extent, shards, low, top_value):
    gain, own = 1.0, jax.random.fold_in(key, 6)
    for dim, parts in shards:
        draws = jnp.exp(jax.random.uniform(jax.random.fold_in(own, dim), (parts,), jnp.float32, low / len(shards), top_value / len(shards)))
        gain = gain * jnp.repeat(draws, extent[dim] // parts).reshape([-1 if axis == dim else 1 for axis in range(len(extent))])
    return gain


def bell_draw(own_key, shape, width, reach, pieces=(), kind=jnp.bfloat16):
    values = width * jax.random.normal(own_key, shape, jnp.float32)
    if pieces:
        values = values * level_of(own_key, shape, pieces, -0.22, 0.18)
    return jnp.clip(values, -reach, reach).astype(kind)


def setup_inputs(seed: int = 0) -> dict:
    seeds = jax.random.split(jax.random.key(seed), 12)
    return {
        "tokens": plant(jax.random.randint(seeds[0], (STEPS, BEAMS), 0, VOCAB), jax.random.fold_in(seeds[0], 1), 0, VOCAB - 1).astype(jnp.int32),
        "parents": draw_parents(jax.random.fold_in(seeds[11], 71), 0),
        "embed_table": draw_embed_table(jax.random.fold_in(seeds[11], 71), 0),
        "norm_gain": jnp.clip(1.0 + 0.18 * jax.random.normal(seeds[3], (2, D), jnp.float32), 0.1, 1.9),
        "weight_in": bell_draw(seeds[4], (2, N_CHAN, N_DP, 3, PIECE, D), D ** -0.5, 0.0625, ((2, 8), (5, 16))),
        "weight_out": bell_draw(seeds[5], (2, N_CHAN, N_DP, PIECE, D), D ** -0.5, 0.0625, ((2, 8), (4, 16))),
        "fir_filters": bell_draw(seeds[6], (GROUPS, TAPS), 0.1, 0.6, ((0, 16),), jnp.float32),
        "mode_poles": jnp.clip(0.3 + 0.69 * jax.random.uniform(seeds[7], (MODES, D), jnp.float32) ** level_of(seeds[7], (MODES, D), ((1, 16),), -0.2, 0.2), 0.3, 0.99),
        "residues": bell_draw(seeds[8], (MODES, D), 0.25, 1.5, ((1, 16),), jnp.float32),
        "fir_cache": bell_draw(seeds[9], (BEAMS, TAPS - 1, D), 1.0, 6.0, ((0, 8), (2, 16))),
        "modal_state": bell_draw(seeds[10], (BEAMS, MODES, D), 2.0, 12.0, ((0, 8), (2, 16)), jnp.float32),
    }


EPSILON = 1e-05

def norm_rows(hidden_in, gain_row):
    values = hidden_in.astype(jnp.float32)
    square_mean = lax.optimization_barrier(jnp.sum(values * values, axis=1, keepdims=True)) / D
    return (values * lax.rsqrt(square_mean + EPSILON) * gain_row[None, :]).astype(jnp.bfloat16)

def fir_mix(tap_rows, cache_rows, product_kv):
    filtered = tap_rows[0][None, :] * product_kv.astype(jnp.float32)
    filtered = filtered + lax.optimization_barrier(jnp.sum(cache_rows.astype(jnp.float32) * tap_rows[1:][None], axis=1))
    updated = jnp.concatenate([product_kv[:, None, :], cache_rows[:, :-1]], axis=1)
    return (filtered, updated)

def modal_mix(mode_poles, residues, state_rows, product_kv):
    updated = mode_poles[None] * state_rows + product_kv.astype(jnp.float32)[:, None, :]
    return (lax.optimization_barrier(jnp.sum(residues[None] * updated, axis=1)), updated)

def hyena_block(hidden_in, gain_row, weight_in_block, weight_out_block, mixing):
    normed = norm_rows(hidden_in, gain_row)
    weight_full = jnp.transpose(weight_in_block, (4, 2, 0, 1, 3)).reshape(D, 3 * D)
    features = jnp.dot(normed, weight_full, preferred_element_type=jnp.float32)
    features = features.astype(jnp.bfloat16).reshape(normed.shape[0], 3, D)
    product_kv = (features[:, 1].astype(jnp.float32) * features[:, 2].astype(jnp.float32)).astype(jnp.bfloat16)
    filtered, memory = mixing(product_kv)
    gated_rows = (features[:, 0].astype(jnp.float32) * filtered).astype(jnp.bfloat16)
    weight_flat = jnp.transpose(weight_out_block, (3, 0, 1, 2)).reshape(D, D)
    outward = jnp.dot(gated_rows, weight_flat, preferred_element_type=jnp.float32)
    outward = outward.astype(jnp.bfloat16)
    return ((hidden_in.astype(jnp.float32) + outward.astype(jnp.float32)).astype(jnp.bfloat16), memory)

def reference(tokens, parents, embed_table, norm_gain, weight_in, weight_out, fir_filters, mode_poles, residues, fir_cache, modal_state):
    tap_rows = jnp.repeat(fir_filters, GROUP, axis=0).T
    cache_now = fir_cache
    state_now = modal_state
    outputs = []
    for step_index in range(STEPS):
        cache_now = cache_now[parents[step_index]]
        state_now = state_now[parents[step_index]]
        hidden_now = embed_table[tokens[step_index]]

        def finite_part(product_kv, cache_rows=cache_now):
            return fir_mix(tap_rows, cache_rows, product_kv)
        hidden_now, cache_now = hyena_block(hidden_now, norm_gain[0], weight_in[0], weight_out[0], finite_part)

        def modal_part(product_kv, state_rows=state_now):
            return modal_mix(mode_poles, residues, state_rows, product_kv)
        hidden_now, state_now = hyena_block(hidden_now, norm_gain[1], weight_in[1], weight_out[1], modal_part)
        outputs.append(hidden_now)
    return (jnp.stack(outputs), cache_now, state_now)
```

```python
import jax
import jax.numpy as jnp
from jax import lax
from jax.experimental import pallas as pl
from jax.experimental.pallas import tpu as pltpu
from jax.sharding import Mesh, PartitionSpec as P

D = 8192
EPSILON = 1e-05
BF = jnp.bfloat16
F32 = jnp.float32
I32 = jnp.int32
HIGH = lax.Precision.HIGHEST
DP = ("y", "xl")
CHAN = ("xh", "z", "c")
XZ = ("xh", "z")
VMEM = pl.BlockSpec(memory_space=pltpu.VMEM)
SMEM = pl.BlockSpec(memory_space=pltpu.SMEM)
ANY = pl.BlockSpec(memory_space=pl.ANY)
LIMIT = 24 * 1024 * 1024
EXTRA = 16


def params(**kw):
    return pltpu.CompilerParams(vmem_limit_bytes=LIMIT, **kw)


def swap(value, axis):
    return lax.ppermute(value, axis, [(0, 1), (1, 0)])


def exchange(value, axes):
    return lax.all_to_all(value, axes, 0, 0, tiled=True)


def sums_kernel(filt_ref, poles_ref, res_ref, state_ref, cache_ref, out_ref, tap_a, tap_b, rows):
    step = pl.program_id(0)

    @pl.when(step == 0)
    def _():
        group = lax.broadcasted_iota(I32, (32, 512), 1) // 16
        spread = (group == lax.broadcasted_iota(I32, (32, 512), 0)).astype(F32)
        taps = lax.dot_general(
            filt_ref[...], spread, (((0,), (0,)), ((), ())),
            preferred_element_type=F32, precision=HIGH,
        )
        place = lax.broadcasted_iota(I32, (128, 512), 0)
        tap_a[...] = pltpu.roll(taps, 127, 0)
        tap_b[...] = jnp.where(place < 126, pltpu.roll(taps, 126, 0), 0.0)
        rows[64:128, :] = jnp.zeros((64, 512), F32)
        rows[64:66, :] = taps[0:2, :]
        poles = poles_ref[...]
        once = res_ref[...] * poles
        twice = once * poles
        rows[66:67, :] = jnp.sum(res_ref[...], axis=0, keepdims=True)
        rows[67:68, :] = jnp.sum(once, axis=0, keepdims=True)
        for b in range(16):
            state = state_ref[b]
            rows[32 + b : 33 + b, :] = jnp.sum(state * once, axis=0, keepdims=True)
            rows[48 + b : 49 + b, :] = jnp.sum(state * twice, axis=0, keepdims=True)

    for s in range(4):
        @pl.when(step == s)
        def _(s=s):
            for k in range(4):
                b = 4 * s + k
                past = cache_ref[k].astype(F32)
                rows[b : b + 1, :] = jnp.sum(past * tap_a[0:127, :], axis=0, keepdims=True)
                rows[16 + b : 17 + b, :] = jnp.sum(past * tap_b[0:127, :], axis=0, keepdims=True)

    @pl.when(step == 3)
    def _():
        out_ref[...] = rows[...].T


def make_sums(filters, poles, residues, state, cache):
    whole = lambda *shape: pl.BlockSpec(shape, lambda s: (0,) * len(shape))
    return pl.pallas_call(
        sums_kernel,
        grid=(4,),
        in_specs=[
            whole(32, 128), whole(16, 512), whole(16, 512), whole(16, 16, 512),
            pl.BlockSpec((4, 127, 512), lambda s: (s, 0, 0)),
        ],
        out_specs=whole(512, 128),
        out_shape=jax.ShapeDtypeStruct((512, 128), F32),
        scratch_shapes=[pltpu.VMEM((128, 512), F32)] * 3,
        compiler_params=params(),
        name="state_sums",
    )(filters, poles, residues, state, cache)


def write_squares(x_own, x_oth, squares):
    total = jnp.sum(x_own * x_own, axis=0, keepdims=True)
    total = total + jnp.sum(x_oth * x_oth, axis=0, keepdims=True)
    high = total.astype(BF).astype(F32)
    low = total - high
    place = lax.broadcasted_iota(I32, (EXTRA, 128), 0)
    squares[...] = jnp.where(place == 0, high, jnp.where(place == 1, low, 0.0)).astype(BF)


def product_in(w_own, w_oth, scaled, squares, out_ref):
    acc = jnp.dot(w_own[0], scaled[0], preferred_element_type=F32)
    acc = acc + jnp.dot(w_oth[0], scaled[1], preferred_element_type=F32)
    out_ref[0, 0:384, :] = acc.astype(BF)
    out_ref[0, 384:400, :] = squares[...]


def embed_kernel(tok_ref, e_own, e_oth, g_own, g_oth, w_own, w_oth, out_ref, x_ref, scaled, squares):
    @pl.when(pl.program_id(0) == 0)
    def _():
        vocab = lax.broadcasted_iota(I32, (512, 128), 0)
        onehot = (vocab == tok_ref[0:1, :]).astype(BF)
        halves = []
        for k, (table, gain) in enumerate(((e_own, g_own), (e_oth, g_oth))):
            x = lax.dot_general(
                table[...], onehot, (((0,), (0,)), ((), ())), preferred_element_type=F32
            )
            x_ref[k] = x.astype(BF)
            scaled[k] = (x * gain[:, 0:1]).astype(BF)
            halves.append(x)
        write_squares(halves[0], halves[1], squares)

    product_in(w_own, w_oth, scaled, squares, out_ref)


W_IN_SPECS = lambda block: [pl.BlockSpec((1, 384, 512), lambda g: (block, g, 0))] * 2
IN_SCRATCH = [pltpu.VMEM((2, 512, 128), BF), pltpu.VMEM((EXTRA, 128), BF)]
COST_IN = pl.CostEstimate(flops=2 * 3072 * 1024 * 128, bytes_accessed=7 << 20, transcendentals=0)
COST_OUT = pl.CostEstimate(flops=2 * 1024 * 1024 * 128, bytes_accessed=5 << 19, transcendentals=0)


def project_embed(tok, e_own, e_oth, g_own, g_oth, w_own, w_oth):
    whole = lambda *shape: pl.BlockSpec(shape, lambda g: (0,) * len(shape))
    return pl.pallas_call(
        embed_kernel,
        grid=(8,),
        in_specs=[
            whole(1, 128), whole(512, 512), whole(512, 512), whole(512, 8), whole(512, 8),
            *W_IN_SPECS(0),
        ],
        out_specs=[pl.BlockSpec((1, 400, 128), lambda g: (g, 0, 0)), whole(2, 512, 128)],
        out_shape=[
            jax.ShapeDtypeStruct((8, 400, 128), BF),
            jax.ShapeDtypeStruct((2, 512, 128), BF),
        ],
        scratch_shapes=IN_SCRATCH,
        compiler_params=params(),
        cost_estimate=COST_IN,
        name="embed_project",
    )(tok, e_own, e_oth, g_own, g_oth, w_own, w_oth)


def gather_rows(c, a_ref, k):
    start = pl.multiple_of((c ^ k) * 64, 64)
    return jnp.concatenate([a_ref[i, pl.ds(start, 64), :] for i in range(8)], axis=0)


def in_kernel(c_ref, a_ref, g_own, g_oth, w_own, w_oth, out_ref, scaled, squares):
    @pl.when(pl.program_id(0) == 0)
    def _():
        halves = []
        for k, gain in enumerate((g_own, g_oth)):
            x = gather_rows(c_ref[0], a_ref, k).astype(F32)
            scaled[k] = (x * gain[:, 1:2]).astype(BF)
            halves.append(x)
        write_squares(halves[0], halves[1], squares)

    product_in(w_own, w_oth, scaled, squares, out_ref)


def project_in(where, rows, g_own, g_oth, w_own, w_oth):
    whole = lambda *shape: pl.BlockSpec(shape, lambda g: (0,) * len(shape))
    return pl.pallas_call(
        in_kernel,
        grid=(8,),
        in_specs=[SMEM, whole(8, 128, 128), whole(512, 8), whole(512, 8), *W_IN_SPECS(1)],
        out_specs=pl.BlockSpec((1, 400, 128), lambda g: (g, 0, 0)),
        out_shape=jax.ShapeDtypeStruct((8, 400, 128), BF),
        scratch_shapes=IN_SCRATCH,
        compiler_params=params(),
        cost_estimate=COST_IN,
        name="norm_project",
    )(where, rows, g_own, g_oth, w_own, w_oth)


def mix_kernel(block, c_ref, r_ref, t_own, t_oth, idx_ref, gated_ref, kv_ref):
    c = c_ref[0]
    total = r_ref[0].astype(F32)
    for g in range(1, 8):
        total = total + r_ref[g].astype(F32)
    squares = total[384:385, :] + total[385:386, :]
    feats = (total[0:384, :] * lax.rsqrt(squares / D + EPSILON)).astype(BF).astype(F32)
    kind = lambda m: jnp.concatenate(
        [feats[64 * m : 64 * m + 64, :], feats[192 + 64 * m : 256 + 64 * m, :]], axis=0
    )
    kv = (kind(1) * kind(2)).astype(BF)
    square = lax.broadcasted_iota(I32, (128, 128), 0)
    earlier = (square == idx_ref[2:3, :]).astype(BF)
    onward = (square == idx_ref[3:4, :]).astype(BF)
    kv_before = jnp.dot(kv, earlier, preferred_element_type=F32)
    kv_ref[...] = jnp.dot(kv, onward, preferred_element_type=F32).T.astype(BF)
    parts, first, second = [], [], []
    for k in range(2):
        own = c == k
        acc = jnp.zeros((64, 128), F32)
        for q in range(4):
            sums = jnp.where(own, t_own[q], t_oth[q])
            pick = (square + 128 * q == idx_ref[block : block + 1, :]).astype(F32)
            acc = acc + jnp.dot(sums, pick, preferred_element_type=F32, precision=HIGH)
            if q == 0:
                first.append(sums[:, 64 + 2 * block : 65 + 2 * block])
                second.append(sums[:, 65 + 2 * block : 66 + 2 * block])
        parts.append(acc)
    first, second = jnp.concatenate(first, axis=0), jnp.concatenate(second, axis=0)
    filtered = first * kv.astype(F32) + second * kv_before + jnp.concatenate(parts, axis=0)
    gated = (kind(0) * filtered).astype(BF)
    for i in range(8):
        gated_ref[i] = gated


def mix(block, where, received, t_own, t_oth, idx):
    return pl.pallas_call(
        lambda *refs: mix_kernel(block, *refs),
        in_specs=[SMEM, VMEM, VMEM, VMEM, VMEM],
        out_specs=[VMEM, VMEM],
        out_shape=[
            jax.ShapeDtypeStruct((8, 128, 128), BF),
            jax.ShapeDtypeStruct((128, 128), BF),
        ],
        compiler_params=params(),
        name="mix",
    )(where, received, t_own, t_oth, idx)


def out_kernel(c_ref, a_ref, w_own, w_oth, out_ref, rows):
    @pl.when(pl.program_id(0) == 0)
    def _():
        for k in range(2):
            rows[k] = gather_rows(c_ref[0], a_ref, k)

    acc = jnp.dot(w_own[0], rows[0], preferred_element_type=F32)
    acc = acc + jnp.dot(w_oth[0], rows[1], preferred_element_type=F32)
    for k in range(2):
        out_ref[k] = acc[128 * k : 128 * k + 128, :].astype(BF)


def project_out(block, where, rows, w_own, w_oth):
    whole = lambda *shape: pl.BlockSpec(shape, lambda g: (0,) * len(shape))
    return pl.pallas_call(
        out_kernel,
        grid=(4,),
        in_specs=[SMEM, whole(8, 128, 128)]
        + [pl.BlockSpec((1, 256, 512), lambda g: (block, g, 0))] * 2,
        out_specs=pl.BlockSpec((2, 128, 128), lambda g: (g, 0, 0)),
        out_shape=jax.ShapeDtypeStruct((8, 128, 128), BF),
        scratch_shapes=[pltpu.VMEM((2, 512, 128), BF)],
        compiler_params=params(),
        cost_estimate=COST_OUT,
        name="project_out",
    )(where, rows, w_own, w_oth)


def add_up(r_ref):
    total = r_ref[0].astype(F32)
    for g in range(1, 8):
        total = total + r_ref[g].astype(F32)
    return total.astype(BF).astype(F32)


def residual_kernel(c_ref, r_ref, x_ref, out_ref):
    outward = add_up(r_ref)
    start = pl.multiple_of(c_ref[1] * 64, 64)
    before = jnp.concatenate(
        [x_ref[c_ref[0] ^ k, pl.ds(start, 64), :] for k in range(2)], axis=0
    )
    hidden = (before.astype(F32) + outward).astype(BF)
    for i in range(8):
        out_ref[i] = hidden


def residual(where, received, embedded):
    return pl.pallas_call(
        residual_kernel,
        in_specs=[SMEM, VMEM, VMEM],
        out_specs=VMEM,
        out_shape=jax.ShapeDtypeStruct((8, 128, 128), BF),
        compiler_params=params(),
        name="residual",
    )(where, received, embedded)


def last_kernel(c_ref, r_ref, h_ref, kv0_ref, kv1_ref, keep_ref, send_ref):
    hidden = (h_ref[0].astype(F32) + add_up(r_ref)).astype(BF).astype(F32).T
    first = c_ref[0] == 0
    for k, rows in enumerate((hidden, kv0_ref[...].astype(F32), kv1_ref[...].astype(F32))):
        low, high = rows[:, 0:64], rows[:, 64:128]
        keep_ref[k] = jnp.where(first, low, high).astype(BF)
        send_ref[k] = jnp.where(first, high, low).astype(BF)


def last(where, received, hidden, kv0, kv1):
    whole = lambda *shape: pl.BlockSpec(shape, lambda g: (0,) * len(shape))
    return pl.pallas_call(
        last_kernel,
        grid=(1,),
        in_specs=[
            SMEM, whole(8, 128, 128), pl.BlockSpec((1, 128, 128), lambda g: (0, 0, 0)),
            whole(128, 128), whole(128, 128),
        ],
        out_specs=[whole(3, 128, 64)] * 2,
        out_shape=[jax.ShapeDtypeStruct((3, 128, 64), BF)] * 2,
        compiler_params=params(),
        name="last",
    )(where, received, hidden, kv0, kv1)


def arrange_kernel(c_ref, keep_ref, got_ref, out_ref):
    first = c_ref[0] == 0
    for k in range(3):
        keep, got = keep_ref[k].astype(F32), got_ref[k].astype(F32)
        for half in range(2):
            rows = jnp.where(first == (half == 0), keep, got).astype(BF)
            for q in range(4):
                out_ref[4 * half + q, 32 * k : 32 * k + 32, :] = rows[32 * q : 32 * q + 32, :]


def arrange(where, keep, got):
    return pl.pallas_call(
        arrange_kernel,
        in_specs=[SMEM, VMEM, VMEM],
        out_specs=VMEM,
        out_shape=jax.ShapeDtypeStruct((8, 96, 64), BF),
        compiler_params=params(),
        name="arrange",
    )(where, keep, got)


def reorder_kernel(pick_ref, own_ref, oth_ref, out_ref, held, ready, sem_in, sem_out):
    for b in range(16):
        row = pick_ref[0, b]

        @pl.when(pick_ref[1, b] == 1)
        def _():
            pltpu.make_async_copy(own_ref.at[row], held.at[b], sem_in.at[b]).start()

        @pl.when(pick_ref[1, b] == 0)
        def _():
            pltpu.make_async_copy(oth_ref.at[row], held.at[b], sem_in.at[b]).start()

    for b in range(16):
        pltpu.make_async_copy(own_ref.at[0], held.at[b], sem_in.at[b]).wait()
        past = held[b].astype(F32)
        moved = jnp.concatenate([past[0:2, :], past[0:125, :]], axis=0)
        ready[b] = moved.astype(BF)
        pltpu.make_async_copy(ready.at[b], out_ref.at[b], sem_out.at[b]).start()
    for b in range(16):
        pltpu.make_async_copy(ready.at[b], out_ref.at[b], sem_out.at[b]).wait()


def reorder(pick, own, oth):
    return pl.pallas_call(
        reorder_kernel,
        in_specs=[SMEM, ANY, ANY],
        out_specs=ANY,
        out_shape=jax.ShapeDtypeStruct((16, 127, 512), BF),
        scratch_shapes=[
            pltpu.VMEM((16, 127, 512), BF),
            pltpu.VMEM((16, 127, 512), BF),
            pltpu.SemaphoreType.DMA((16,)),
            pltpu.SemaphoreType.DMA((16,)),
        ],
        compiler_params=params(),
        cost_estimate=pl.CostEstimate(flops=0, bytes_accessed=4 << 20, transcendentals=0),
        name="reorder",
    )(pick, own, oth)


def final_kernel(pick_ref, r_ref, poles_ref, own_ref, oth_ref, fir_ref, hid_ref, fir_out, state_ref):
    wide = lambda start: jnp.concatenate(
        [r_ref[i, start : start + 16, :].astype(F32) for i in range(8)], axis=1
    )
    for t in range(2):
        hid_ref[t] = wide(16 * t).astype(BF)
    before, now = wide(32), wide(48)
    place = lax.broadcasted_iota(I32, (16, 512), 0)
    for b in range(16):
        old = fir_ref[b].astype(F32)
        fresh = jnp.where(place == 0, now[b : b + 1, :], before[b : b + 1, :])
        fir_out[b] = jnp.where(place < 2, fresh, old).astype(BF)
    before, now = wide(64), wide(80)
    poles = poles_ref[...]
    for b in range(16):
        row = pick_ref[0, b]
        old = jnp.where(pick_ref[1, b] == 1, own_ref[row], oth_ref[row])
        state_ref[b] = poles * (poles * old + before[b : b + 1, :]) + now[b : b + 1, :]


def final(pick, received, poles, own, oth, fir):
    whole = lambda *shape: pl.BlockSpec(shape, lambda g: (0,) * len(shape))
    return pl.pallas_call(
        final_kernel,
        grid=(1,),
        in_specs=[
            SMEM, whole(8, 96, 64), whole(16, 512), whole(16, 16, 512), whole(16, 16, 512),
            whole(16, 16, 512),
        ],
        out_specs=[whole(2, 16, 512), whole(16, 16, 512), whole(16, 16, 512)],
        out_shape=[
            jax.ShapeDtypeStruct((2, 16, 512), BF),
            jax.ShapeDtypeStruct((16, 127, 512), BF),
            jax.ShapeDtypeStruct((16, 16, 512), F32),
        ],
        input_output_aliases={5: 1},
        compiler_params=params(),
        name="final",
    )(pick, received, poles, own, oth, fir)


def indices(parents, dp, c):
    beams = jnp.arange(128, dtype=I32)
    composed = jnp.sum(
        jnp.where(parents[1][None, :] == beams[:, None], parents[0][:, None], 0), axis=0
    )
    chosen = jnp.stack([parents[0], parents[1], composed])
    mine = lax.dynamic_slice_in_dim(composed, dp * 16, 16, 0)
    pick = jnp.stack([mine % 16, (mine // 16 == dp).astype(I32)])
    half = lax.dynamic_slice_in_dim(chosen, c * 64, 64, 1) - c * 64
    p0, p1, pp = half[0].reshape(4, 16), half[1].reshape(4, 16), half[2].reshape(4, 16)
    sums_row = lambda beam, kind: beam // 16 * 128 + kind * 16 + beam % 16
    column = lambda beam, t: beam // 16 * 32 + t * 16 + beam % 16
    both = lambda a, b: jnp.stack([a, b], axis=1).reshape(128)
    here = jnp.arange(64, dtype=I32).reshape(4, 16)
    rows = [
        both(sums_row(p0, 0), sums_row(pp, 1)),
        both(sums_row(p0, 2), sums_row(pp, 3)),
        both(jnp.full_like(p1, -1), column(p1, 0)),
        both(column(p1, 0), column(here, 1)),
    ]
    return jnp.stack(rows + [rows[0]] * 4), pick


def local(
    tokens, parents, embed_table, norm_gain, weight_in, weight_out, fir_filters, mode_poles,
    residues, fir_cache, modal_state,
):
    dp = lax.axis_index(DP).astype(I32)
    c = lax.axis_index("c").astype(I32)
    where = jnp.stack([c, dp])
    w_in = weight_in.reshape(2, 3072, 512)
    w_out = weight_out.reshape(2, 1024, 512)

    slot = (jnp.arange(4, dtype=I32) == dp % 4).astype(I32)
    row = (slot[:, None] * tokens.reshape(1, 32)).reshape(1, 128)
    got = exchange(jnp.broadcast_to(row[None], (8, 1, 128)), DP)
    tok = jnp.sum(lax.dynamic_slice_in_dim(got, c * 4, 4, 0), axis=0)

    gains = jnp.concatenate([norm_gain, jnp.zeros((6, 512), F32)], axis=0)
    e_oth = swap(embed_table, "c")
    g_own = gains.T
    g_oth = swap(g_own, "c")
    w_in_oth = swap(w_in, "c")
    w_out_oth = swap(w_out, "c")
    cache_oth = swap(fir_cache, "xl")
    state_oth = swap(modal_state, "xl")
    idx, pick = indices(parents, dp, c)

    sums = make_sums(fir_filters, mode_poles, residues, modal_state, fir_cache)
    sums = exchange(sums.reshape(8, 64, 128), DP)
    t_own = lax.dynamic_slice_in_dim(sums, c * 4, 4, 0)
    t_oth = swap(lax.dynamic_slice_in_dim(sums, 4 - c * 4, 4, 0), "c")

    partial, embedded = project_embed(tok, embed_table, e_oth, g_own, g_oth, w_in, w_in_oth)
    gated, kv0 = mix(0, where, exchange(partial, XZ), t_own, t_oth, idx)
    partial = project_out(0, where, exchange(gated, DP), w_out, w_out_oth)
    hidden = residual(where, exchange(partial, XZ), embedded)
    partial = project_in(where, exchange(hidden, DP), g_own, g_oth, w_in, w_in_oth)
    gated, kv1 = mix(1, where, exchange(partial, XZ), t_own, t_oth, idx)
    partial = project_out(1, where, exchange(gated, DP), w_out, w_out_oth)
    keep, send = last(where, exchange(partial, XZ), hidden, kv0, kv1)
    moved = exchange(arrange(where, keep, swap(send, "c")), DP)
    fir_before = reorder(pick, fir_cache, cache_oth)
    return final(pick, moved, mode_poles, modal_state, state_oth, fir_before)


def solution(mesh):
    fine = Mesh(mesh.devices.reshape(4, 2, 2, 4, 2), ("y", "xl", "xh", "z", "c"))
    return jax.shard_map(
        local,
        mesh=fine,
        in_specs=(
            P(None, DP),
            P(),
            P(None, CHAN),
            P(None, CHAN),
            P(None, None, DP, None, None, CHAN),
            P(None, None, DP, None, CHAN),
            P(CHAN, None),
            P(None, CHAN),
            P(None, CHAN),
            P(DP, None, CHAN),
            P(DP, None, CHAN),
        ),
        out_specs=(P(None, DP, CHAN), P(DP, None, CHAN), P(DP, None, CHAN)),
        check_vma=False,
    )
```

```python
import jax
import jax.numpy as jnp
from jax import lax
from jax.experimental import pallas as pl
from jax.experimental.pallas import tpu as pltpu
from jax.sharding import Mesh, PartitionSpec as P

D = 8192
EPSILON = 1e-05
BF = jnp.bfloat16
F32 = jnp.float32
I32 = jnp.int32
HIGH = lax.Precision.HIGHEST
DP = ("y", "xl")
CHAN = ("xh", "z", "c")
XZ = ("xh", "z")
SMEM = pl.BlockSpec(memory_space=pltpu.SMEM)
HBM = pl.BlockSpec(memory_space=pltpu.HBM)
LARGE = 64 * 1024 * 1024
CHUNKS = (48, 29, 48)
EXTRA = 16


def params():
    return pltpu.CompilerParams(vmem_limit_bytes=LARGE)


def whole(*shape):
    return pl.BlockSpec(shape, lambda g: (0,) * len(shape))


def swap(value, axis):
    return lax.ppermute(value, axis, [(0, 1), (1, 0)])


def exchange(value, axes):
    return lax.all_to_all(value, axes, 0, 0, tiled=True)


def sums_kernel(
    c_ref, tok_ref, filt_ref, poles_ref, res_ref, state_ref, cache_ref, out_ref, *refs
):
    pieces, (sent_ref, taps, rows, held, sems, sem_out) = refs[: len(CHUNKS)], refs[len(CHUNKS) :]
    copies = []
    for k in range(4):
        size = 32 if k < 3 else 31
        piece = pl.ds(32 * k, size)
        copies.append(pltpu.make_async_copy(cache_ref.at[piece], held.at[piece], sems.at[k]))
        copies[-1].start()
    group = lax.broadcasted_iota(I32, (32, 512), 1) // 16
    spread = (group == lax.broadcasted_iota(I32, (32, 512), 0)).astype(F32)
    taps[0:128, :] = lax.dot_general(
        filt_ref[...], spread, (((0,), (0,)), ((), ())),
        preferred_element_type=F32, precision=HIGH,
    )
    taps[128:136, :] = jnp.zeros((8, 512), F32)
    rows[64:128, :] = jnp.zeros((64, 512), F32)
    rows[64:66, :] = taps[0:2, :]
    once = res_ref[...] * poles_ref[...]
    twice = once * poles_ref[...]
    rows[66:67, :] = jnp.sum(res_ref[...], axis=0, keepdims=True)
    rows[67:68, :] = jnp.sum(once, axis=0, keepdims=True)
    for b in range(16):
        state = state_ref[b]
        rows[32 + b : 33 + b, :] = jnp.sum(state * once, axis=0, keepdims=True)
        rows[48 + b : 49 + b, :] = jnp.sum(state * twice, axis=0, keepdims=True)
        sent_ref[b] = state.astype(BF)

    def add_tap(s, sums):
        past = held[s].astype(F32)
        return (
            sums[0] + past * taps[pl.ds(s + 1, 1), :],
            sums[1] + past * taps[pl.ds(s + 2, 1), :],
        )

    sums = (jnp.zeros((16, 512), F32),) * 2
    outs, start, size = [], 0, 0
    for k in range(4):
        copies[k].wait()
        while len(outs) < len(CHUNKS) and start + CHUNKS[len(outs)] <= 32 * k + 32:
            size = CHUNKS[len(outs)]
            outs.append(
                pltpu.make_async_copy(
                    held.at[start : start + size], pieces[len(outs)], sem_out.at[len(outs)]
                )
            )
            outs[-1].start()
            start += size
        sums = lax.fori_loop(32 * k, 32 * k + (32 if k < 3 else 31), add_tap, sums, unroll=True)
    rows[0:16, :] = sums[0]
    rows[16:32, :] = sums[1]
    columns = rows[...].T
    lane = lax.broadcasted_iota(I32, (8, 128), 1)
    start = (c_ref[1] % 4) * 32
    tok = jnp.zeros((8, 128), I32)
    for t in range(2):
        for b in range(16):
            tok = jnp.where(lane == start + 16 * t + b, tok_ref[t, b], tok)
    tok = tok.astype(F32)
    for i in range(8):
        out_ref[i, 0:64, :] = columns[64 * i : 64 * i + 64, :]
        out_ref[i, 64:72, :] = tok
    for copy in outs:
        copy.wait()


def make_sums(where, tokens, filters, poles, residues, state, cache):
    return pl.pallas_call(
        sums_kernel,
        grid=(1,),
        in_specs=[
            SMEM, SMEM, whole(32, 128), whole(16, 512), whole(16, 512), whole(16, 16, 512), HBM,
        ],
        out_specs=[whole(8, 72, 128)] + [HBM] * len(CHUNKS) + [whole(16, 16, 512)],
        out_shape=[jax.ShapeDtypeStruct((8, 72, 128), F32)]
        + [jax.ShapeDtypeStruct((size, 16, 512), BF) for size in CHUNKS + (16,)],
        scratch_shapes=[
            pltpu.VMEM((136, 512), F32),
            pltpu.VMEM((128, 512), F32),
            pltpu.VMEM((127, 16, 512), BF),
            pltpu.SemaphoreType.DMA((4,)),
            pltpu.SemaphoreType.DMA((len(CHUNKS),)),
        ],
        compiler_params=params(),
        name="state_sums",
    )(where, tokens, filters, poles, residues, state, cache)


def index_kernel(c_ref, par_ref, out_ref):
    base = c_ref[0] * 64
    lane = lax.broadcasted_iota(I32, (1, 128), 1)
    fir, onward = jnp.zeros((1, 128), I32), lane
    earlier = jnp.full((1, 128), -1, I32)
    place = lambda beam, wide: (beam >> 4) * wide + (beam & 15)
    for j in range(64):
        after = par_ref[1, base + j]
        old, older = par_ref[0, base + j] - base, par_ref[0, after] - base
        source = place(after - base, 32)
        first = lane == j // 16 * 32 + j % 16
        second = lane == j // 16 * 32 + 16 + j % 16
        fir = jnp.where(first, place(old, 128), jnp.where(second, place(older, 128) + 16, fir))
        earlier = jnp.where(second, source, earlier)
        onward = jnp.where(first, source, onward)
    out_ref[0:1, :] = fir
    out_ref[1:2, :] = fir + 32
    out_ref[2:3, :] = earlier
    out_ref[3:4, :] = onward
    out_ref[4:8, :] = jnp.zeros((4, 128), I32)


def indices(where, parents):
    return pl.pallas_call(
        index_kernel,
        grid=(1,),
        in_specs=[SMEM, SMEM],
        out_specs=whole(8, 128),
        out_shape=jax.ShapeDtypeStruct((8, 128), I32),
        compiler_params=params(),
        name="indices",
    )(where, parents)


def turn_kernel(own_ref, oth_ref, out_ref):
    for k, table in enumerate((own_ref, oth_ref)):
        out_ref[k] = table[...].T


def turn(own, oth):
    return pl.pallas_call(
        turn_kernel,
        grid=(1,),
        in_specs=[whole(512, 512)] * 2,
        out_specs=whole(2, 512, 512),
        out_shape=jax.ShapeDtypeStruct((2, 512, 512), BF),
        compiler_params=params(),
        name="turn",
    )(own, oth)


def weights(block, rows):
    return [pl.BlockSpec((1, rows // 2, 512), lambda g: (block, g, 0))] * 2


def squares_rows(x_own, x_oth):
    total = jnp.sum(x_own * x_own, axis=0, keepdims=True)
    total = total + jnp.sum(x_oth * x_oth, axis=0, keepdims=True)
    high = total.astype(BF).astype(F32)
    low = total - high
    place = lax.broadcasted_iota(I32, (EXTRA, 128), 0)
    return jnp.where(place == 0, high, jnp.where(place == 1, low, 0.0)).astype(BF)


def column(gain_ref, k):
    return jnp.broadcast_to(gain_ref[k : k + 1, :], (8, 512)).T[:, 0:1]


def hand_out(acc, rows, where_ref, outs, spread):
    half = pl.program_id(0) ^ where_ref[2]
    spread[...] = acc
    for s in range(4):
        start = pl.multiple_of(((where_ref[3] + s) & 3) * rows, rows)
        outs[s][half, 0:rows, :] = spread[pl.ds(start, rows), :]
    return half


def product_in(where_ref, w_own, w_oth, scaled, squares, spread, outs):
    acc = jnp.dot(w_own[0], scaled[0], preferred_element_type=F32)
    acc = (acc + jnp.dot(w_oth[0], scaled[1], preferred_element_type=F32)).astype(BF)
    half = hand_out(acc, 384, where_ref, outs, spread)
    for out in outs:
        out[half, 384:400, :] = squares[...]


def embed_kernel(
    c_ref, got_ref, tables, g_own, g_oth, w_own, w_oth, *refs
):
    *outs, x_ref, send_ref, scaled, squares, spread = refs

    @pl.when(pl.program_id(0) == 0)
    def _():
        c = c_ref[0]
        tok = jnp.zeros((8, 128), F32)
        for q in range(4):
            tok = tok + got_ref[c * 4 + q, 64:72, :]
            send_ref[q] = got_ref[4 - c * 4 + q, 0:64, :]
        vocab = lax.broadcasted_iota(I32, (512, 128), 0)
        onehot = (vocab == tok[0:1, :].astype(I32)).astype(BF)
        halves = []
        for k, gain in enumerate((g_own, g_oth)):
            x = jnp.dot(tables[k], onehot, preferred_element_type=F32)
            x_ref[k] = x.astype(BF)
            scaled[k] = (x * column(gain, 0)).astype(BF)
            halves.append(x)
        squares[...] = squares_rows(*halves)

    product_in(c_ref, w_own, w_oth, scaled, squares, spread, outs)


IN_SCRATCH = [
    pltpu.VMEM((2, 512, 128), BF), pltpu.VMEM((EXTRA, 128), BF), pltpu.VMEM((1536, 128), BF)
]
IN_SHAPE = [jax.ShapeDtypeStruct((2, 400, 128), BF)] * 4
IN_SPECS = [whole(2, 400, 128)] * 4
COST_IN = pl.CostEstimate(flops=2 * 3072 * 1024 * 128, bytes_accessed=7 << 20, transcendentals=0)
COST_OUT = pl.CostEstimate(flops=2 * 1024 * 1024 * 128, bytes_accessed=5 << 19, transcendentals=0)


def project_embed(where, got, tables, g_own, g_oth, w_own, w_oth):
    return pl.pallas_call(
        embed_kernel,
        grid=(2,),
        in_specs=[
            SMEM, whole(8, 72, 128), whole(2, 512, 512), whole(2, 512), whole(2, 512),
            *weights(0, 3072),
        ],
        out_specs=[*IN_SPECS, whole(2, 512, 128), whole(4, 64, 128)],
        out_shape=[
            *IN_SHAPE,
            jax.ShapeDtypeStruct((2, 512, 128), BF),
            jax.ShapeDtypeStruct((4, 64, 128), F32),
        ],
        scratch_shapes=IN_SCRATCH,
        compiler_params=params(),
        cost_estimate=COST_IN,
        name="embed_project",
    )(where, got, tables, g_own, g_oth, w_own, w_oth)


def gather_rows(c, a_ref, k):
    start = pl.multiple_of((c ^ k) * 64, 64)
    return jnp.concatenate([a_ref[i, pl.ds(start, 64), :] for i in range(8)], axis=0)


def in_kernel(c_ref, a_ref, g_own, g_oth, w_own, w_oth, *refs):
    *outs, scaled, squares, spread = refs

    @pl.when(pl.program_id(0) == 0)
    def _():
        halves = []
        for k, gain in enumerate((g_own, g_oth)):
            x = gather_rows(c_ref[0], a_ref, k).astype(F32)
            scaled[k] = (x * column(gain, 1)).astype(BF)
            halves.append(x)
        squares[...] = squares_rows(*halves)

    product_in(c_ref, w_own, w_oth, scaled, squares, spread, outs)


def project_in(where, rows, g_own, g_oth, w_own, w_oth):
    return pl.pallas_call(
        in_kernel,
        grid=(2,),
        in_specs=[
            SMEM, whole(8, 128, 128), whole(2, 512), whole(2, 512), *weights(1, 3072),
        ],
        out_specs=IN_SPECS,
        out_shape=IN_SHAPE,
        scratch_shapes=IN_SCRATCH,
        compiler_params=params(),
        cost_estimate=COST_IN,
        name="norm_project",
    )(where, rows, g_own, g_oth, w_own, w_oth)


def add_up(terms):
    *near, far = terms
    total = far[...].astype(F32)
    for term in near:
        total = total + term[0].astype(F32)
    return total


def terms_specs(rows):
    return [pl.BlockSpec((1, rows, 128), lambda g: (0, 0, 0))] * 4 + [whole(rows, 128)]


def mix_kernel(block, c_ref, *refs):
    t_own, t_oth, idx_ref, gated_ref, kv_ref = refs[5:]
    c = c_ref[0]
    total = add_up(refs[:5])
    squares = total[384:385, :] + total[385:386, :]
    feats = (total[0:384, :] * lax.rsqrt(squares / D + EPSILON)).astype(BF).astype(F32)
    kind = lambda m: jnp.concatenate(
        [feats[64 * m : 64 * m + 64, :], feats[192 + 64 * m : 256 + 64 * m, :]], axis=0
    )
    kv = (kind(1) * kind(2)).astype(BF)
    square = lax.broadcasted_iota(I32, (128, 128), 0)
    earlier = (square == idx_ref[2:3, :]).astype(BF)
    onward = (square == idx_ref[3:4, :]).astype(BF)
    kv_before = jnp.dot(kv, earlier, preferred_element_type=F32)
    kv_ref[...] = jnp.dot(kv, onward, preferred_element_type=F32).T.astype(BF)
    parts, first, second = [], [], []
    for k in range(2):
        own = c == k
        acc = jnp.zeros((64, 128), F32)
        for q in range(4):
            sums = jnp.where(own, t_own[c * 4 + q, 0:64, :], t_oth[q])
            pick = (square + 128 * q == idx_ref[block : block + 1, :]).astype(F32)
            acc = acc + jnp.dot(sums, pick, preferred_element_type=F32, precision=HIGH)
            if q == 0:
                first.append(sums[:, 64 + 2 * block : 65 + 2 * block])
                second.append(sums[:, 65 + 2 * block : 66 + 2 * block])
        parts.append(acc)
    first, second = jnp.concatenate(first, axis=0), jnp.concatenate(second, axis=0)
    filtered = first * kv.astype(F32) + second * kv_before + jnp.concatenate(parts, axis=0)
    gated = (kind(0) * filtered).astype(BF)
    for i in range(8):
        gated_ref[i] = gated


def mix(block, where, received, t_own, t_oth, idx):
    return pl.pallas_call(
        lambda *refs: mix_kernel(block, *refs),
        grid=(1,),
        in_specs=[
            SMEM, *terms_specs(400), whole(8, 72, 128), whole(4, 64, 128), whole(8, 128)
        ],
        out_specs=[whole(8, 128, 128), whole(128, 128)],
        out_shape=[
            jax.ShapeDtypeStruct((8, 128, 128), BF),
            jax.ShapeDtypeStruct((128, 128), BF),
        ],
        compiler_params=params(),
        name="mix",
    )(where, *received, t_own, t_oth, idx)


def out_kernel(c_ref, a_ref, w_own, w_oth, *refs):
    *outs, rows, spread = refs

    @pl.when(pl.program_id(0) == 0)
    def _():
        for k in range(2):
            rows[k] = gather_rows(c_ref[0], a_ref, k)

    acc = jnp.dot(w_own[0], rows[0], preferred_element_type=F32)
    acc = (acc + jnp.dot(w_oth[0], rows[1], preferred_element_type=F32)).astype(BF)
    hand_out(acc, 128, c_ref, outs, spread)


def project_out(block, where, rows, w_own, w_oth):
    return pl.pallas_call(
        out_kernel,
        grid=(2,),
        in_specs=[SMEM, whole(8, 128, 128), *weights(block, 1024)],
        out_specs=[whole(2, 128, 128)] * 4,
        out_shape=[jax.ShapeDtypeStruct((2, 128, 128), BF)] * 4,
        scratch_shapes=[pltpu.VMEM((2, 512, 128), BF), pltpu.VMEM((512, 128), BF)],
        compiler_params=params(),
        cost_estimate=COST_OUT,
        name="project_out",
    )(where, rows, w_own, w_oth)


def residual_kernel(c_ref, *refs):
    x_ref, out_ref = refs[5:]
    outward = add_up(refs[:5]).astype(BF).astype(F32)
    start = pl.multiple_of(c_ref[1] * 64, 64)
    before = jnp.concatenate(
        [x_ref[c_ref[0] ^ k, pl.ds(start, 64), :] for k in range(2)], axis=0
    )
    hidden = (before.astype(F32) + outward).astype(BF)
    for i in range(8):
        out_ref[i] = hidden


def residual(where, received, embedded):
    return pl.pallas_call(
        residual_kernel,
        grid=(1,),
        in_specs=[SMEM, *terms_specs(128), whole(2, 512, 128)],
        out_specs=whole(8, 128, 128),
        out_shape=jax.ShapeDtypeStruct((8, 128, 128), BF),
        compiler_params=params(),
        name="residual",
    )(where, *received, embedded)


def last_kernel(c_ref, *refs):
    h_ref, kv0_ref, kv1_ref, keep_ref, send_ref = refs[5:]
    outward = add_up(refs[:5]).astype(BF).astype(F32)
    hidden = (h_ref[0].astype(F32) + outward).astype(BF).astype(F32).T
    first = c_ref[0] == 0
    kv0, kv1 = kv0_ref[...].astype(F32), kv1_ref[...].astype(F32)
    pair = lambda k: jnp.concatenate(
        [hidden[:, 64 * k : 64 * k + 64], kv0[:, 64 * k : 64 * k + 64]], axis=1
    )
    low, high = pair(0), pair(1)
    keep_ref[0] = jnp.where(first, low, high).astype(BF)
    send_ref[0] = jnp.where(first, high, low).astype(BF)
    turned = pltpu.roll(kv1, 64, 1)
    keep_ref[1] = jnp.where(first, kv1, turned).astype(BF)
    send_ref[1] = jnp.where(first, turned, kv1).astype(BF)


def last(where, received, hidden, kv0, kv1):
    return pl.pallas_call(
        last_kernel,
        grid=(1,),
        in_specs=[
            SMEM, *terms_specs(128), pl.BlockSpec((1, 128, 128), lambda g: (0, 0, 0)),
            whole(128, 128), whole(128, 128),
        ],
        out_specs=[whole(2, 128, 128)] * 2,
        out_shape=[jax.ShapeDtypeStruct((2, 128, 128), BF)] * 2,
        compiler_params=params(),
        name="last",
    )(where, *received, hidden, kv0, kv1)


def arrange_kernel(c_ref, keep_ref, got_ref, out_ref):
    first = c_ref[0] == 0
    for k in range(2):
        keep, got = keep_ref[k].astype(F32), got_ref[k].astype(F32)
        for half in range(2):
            rows = jnp.where(first == (half == 0), keep, got).astype(BF)
            for q in range(4):
                out_ref[4 * half + q, 32 * k : 32 * k + 32, :] = rows[32 * q : 32 * q + 32, :]


def arrange(where, keep, got):
    return pl.pallas_call(
        arrange_kernel,
        grid=(1,),
        in_specs=[SMEM, whole(2, 128, 128), whole(2, 128, 128)],
        out_specs=whole(8, 64, 128),
        out_shape=jax.ShapeDtypeStruct((8, 64, 128), BF),
        compiler_params=params(),
        name="arrange",
    )(where, keep, got)


def origin(where_ref, par_ref, b):
    dp = where_ref[1]
    beam = par_ref[0, par_ref[1, dp * 16 + b]]
    return beam & 15, (beam >> 4) == dp


def reorder_kernel(where_ref, par_ref, own_ref, *refs):
    pieces, (out_ref, held, ready, sems, sem_out) = refs[: len(CHUNKS)], refs[len(CHUNKS) :]
    copies = [pltpu.make_async_copy(own_ref.at[0:125], held.at[0, 0:125], sems.at[0])]
    start = 0
    for k, size in enumerate(CHUNKS):
        copies.append(
            pltpu.make_async_copy(pieces[k], held.at[1, start : start + size], sems.at[k + 1])
        )
        start += size
    for copy in copies:
        copy.start()
    held[0, 125:128] = jnp.zeros((3, 16, 512), BF)
    held[1, 125:128] = jnp.zeros((3, 16, 512), BF)
    row = lax.broadcasted_iota(I32, (128, 256), 0)
    col = lax.broadcasted_iota(I32, (128, 256), 1)
    wanted = jnp.zeros((128, 256), I32)
    for b in range(16):
        slot, here = origin(where_ref, par_ref, b)
        wanted = jnp.where((row & 15) == b, slot + jnp.where(here, 0, 16), wanted)
    same_tap = ((col >> 4) & 7) == (row >> 4)
    pick = (same_tap & ((col & 15) + (col >> 7) * 16 == wanted)).astype(BF)
    for copy in copies:
        copy.wait()
    outs = []
    for k in range(16):
        taps = slice(8 * k, 8 * k + 8)
        both = jnp.concatenate(
            [held[0, taps].reshape(128, 512), held[1, taps].reshape(128, 512)], axis=0
        )
        moved = jnp.dot(pick, both, preferred_element_type=F32).astype(BF)
        ready[taps] = moved.reshape(8, 16, 512)
        size = 8 if k < 15 else 5
        outs.append(
            pltpu.make_async_copy(
                ready.at[8 * k : 8 * k + size], out_ref.at[8 * k + 2 : 8 * k + 2 + size],
                sem_out.at[k],
            )
        )
        outs[-1].start()
    for copy in outs:
        copy.wait()


def reorder(where, parents, own, pieces):
    return pl.pallas_call(
        reorder_kernel,
        in_specs=[SMEM, SMEM, HBM] + [HBM] * len(CHUNKS),
        out_specs=HBM,
        out_shape=jax.ShapeDtypeStruct((127, 16, 512), BF),
        scratch_shapes=[
            pltpu.VMEM((2, 128, 16, 512), BF),
            pltpu.VMEM((128, 16, 512), BF),
            pltpu.SemaphoreType.DMA((len(CHUNKS) + 1,)),
            pltpu.SemaphoreType.DMA((16,)),
        ],
        compiler_params=params(),
        cost_estimate=pl.CostEstimate(flops=1 << 29, bytes_accessed=6 << 20, transcendentals=0),
        name="reorder",
    )(where, parents, own, *pieces)


def final_kernel(
    where_ref, par_ref, r_ref, poles_ref, own_ref, oth_ref, fir_ref,
    hid_ref, fir_out, state_ref, fresh, sem,
):
    wide = lambda row, lane: jnp.concatenate(
        [r_ref[i, row : row + 16, :].astype(F32)[:, lane : lane + 64] for i in range(8)], axis=1
    )
    fresh[0] = wide(16, 64).astype(BF)
    fresh[1] = wide(0, 64).astype(BF)
    copy = pltpu.make_async_copy(fresh, fir_out.at[0:2], sem)
    copy.start()
    for t in range(2):
        hid_ref[t] = wide(16 * t, 0).astype(BF)
    before, now = wide(32, 0), wide(48, 0)
    poles = poles_ref[...]
    for b in range(16):
        slot, here = origin(where_ref, par_ref, b)
        old = jnp.where(here, own_ref[slot], oth_ref[slot].astype(F32))
        state_ref[b] = poles * (poles * old + before[b : b + 1, :]) + now[b : b + 1, :]
    copy.wait()


def final(where, parents, received, poles, own, oth, fir):
    return pl.pallas_call(
        final_kernel,
        grid=(1,),
        in_specs=[
            SMEM, SMEM, whole(8, 64, 128), whole(16, 512), whole(16, 16, 512),
            whole(16, 16, 512), HBM,
        ],
        out_specs=[whole(2, 16, 512), HBM, whole(16, 16, 512)],
        out_shape=[
            jax.ShapeDtypeStruct((2, 16, 512), BF),
            jax.ShapeDtypeStruct((127, 16, 512), BF),
            jax.ShapeDtypeStruct((16, 16, 512), F32),
        ],
        scratch_shapes=[pltpu.VMEM((2, 16, 512), BF), pltpu.SemaphoreType.DMA],
        input_output_aliases={6: 1},
        compiler_params=params(),
        name="final",
    )(where, parents, received, poles, own, oth, fir)


def local(
    tokens, parents, embed_table, norm_gain, weight_in, weight_out, fir_filters, mode_poles,
    residues, fir_cache, modal_state,
):
    dp = lax.axis_index(DP).astype(I32)
    c = lax.axis_index("c").astype(I32)
    where = jnp.stack([c, dp, lax.axis_index("xh").astype(I32), lax.axis_index("z").astype(I32)])
    w_in = weight_in.reshape(2, 3072, 512)
    w_out = weight_out.reshape(2, 1024, 512)
    cache = jnp.transpose(fir_cache, (1, 0, 2))
    e_oth = swap(embed_table, "c")
    g_oth = swap(norm_gain, "c")
    sums, *pieces = make_sums(
        where, tokens, fir_filters, mode_poles, residues, modal_state, cache
    )
    w_in, w_out, e_oth, sums = lax.optimization_barrier((w_in, w_out, e_oth, sums))
    w_in_oth = swap(w_in, "c")
    w_out_oth = swap(w_out, "c")
    moved = []

    def send(trigger):
        piece, trigger, moved[-1:] = lax.optimization_barrier(
            (pieces[len(moved)], trigger, moved[-1:])
        )
        moved.append(swap(piece, "xl"))
        return trigger

    def scatter(terms):
        terms = list(terms)
        for s in (2, 1, 3):
            terms[s] = lax.ppermute(terms[s], "z", [(z, (z + s) % 4) for z in range(4)])
        far = sum(term[1].astype(F32) for term in terms).astype(BF)
        far, moved[-1] = lax.optimization_barrier((far, moved[-1]))
        return *terms, swap(far, "xh")

    idx = indices(where, parents)
    tables = turn(embed_table, e_oth)
    got, idx, tables = lax.optimization_barrier((exchange(sums, DP), idx, tables))
    *partial, embedded, t_send = project_embed(
        where, send(got), tables, norm_gain, g_oth, w_in, w_in_oth
    )
    t_oth = swap(t_send, "c")
    gated, kv0 = mix(0, where, scatter(partial), got, t_oth, idx)
    partial = project_out(
        0, where, send(exchange(gated, DP)), w_out, w_out_oth
    )
    hidden = residual(where, scatter(partial), embedded)
    partial = project_in(
        where, send(exchange(hidden, DP)), norm_gain, g_oth, w_in, w_in_oth
    )
    gated, kv1 = mix(1, where, scatter(partial), got, t_oth, idx)
    partial = project_out(
        1, where, send(exchange(gated, DP)), w_out, w_out_oth
    )
    keep, crossing = last(where, scatter(partial), hidden, kv0, kv1)
    received = exchange(arrange(where, keep, swap(crossing, "c")), DP)
    *moved, state_oth = moved
    fir_before = reorder(where, parents, cache, moved)
    hidden_out, fir_next, state_next = final(
        where, parents, received, mode_poles, modal_state, state_oth, fir_before
    )
    return hidden_out, jnp.transpose(fir_next, (1, 0, 2)), state_next


def solution(mesh):
    fine = Mesh(mesh.devices.reshape(4, 2, 2, 4, 2), ("y", "xl", "xh", "z", "c"))
    return jax.shard_map(
        local,
        mesh=fine,
        in_specs=(
            P(None, DP),
            P(),
            P(None, CHAN),
            P(None, CHAN),
            P(None, None, DP, None, None, CHAN),
            P(None, None, DP, None, CHAN),
            P(CHAN, None),
            P(None, CHAN),
            P(None, CHAN),
            P(DP, None, CHAN),
            P(DP, None, CHAN),
        ),
        out_specs=(P(None, DP, CHAN), P(DP, None, CHAN), P(DP, None, CHAN)),
        check_vma=False,
    )
```

```python
import jax
import jax.numpy as jnp
from jax import lax
from jax.experimental import pallas as pl
from jax.experimental.pallas import tpu as pltpu
from jax.sharding import Mesh, PartitionSpec as P

D = 8192
EPSILON = 1e-05
BF = jnp.bfloat16
F32 = jnp.float32
I32 = jnp.int32
HIGH = lax.Precision.HIGHEST
DP = ("y", "xl")
CHAN = ("xh", "z", "c")
XZ = ("xh", "z")
SMEM = pl.BlockSpec(memory_space=pltpu.SMEM)
HBM = pl.BlockSpec(memory_space=pltpu.HBM)
LARGE = 62 * 1024 * 1024 + 512 * 1024
SMALL = 8 * 1024 * 1024
CHUNKS = (48, 29, 48)
EXTRA = 16


def params(limit=LARGE):
    return pltpu.CompilerParams(vmem_limit_bytes=limit)


def whole(*shape):
    return pl.BlockSpec(shape, lambda g: (0,) * len(shape))


def swap(value, axis):
    return lax.ppermute(value, axis, [(0, 1), (1, 0)])


def exchange(value, axes):
    return lax.all_to_all(value, axes, 0, 0, tiled=True)


def sums_kernel(
    c_ref, tok_ref, filt_ref, poles_ref, res_ref, state_ref, cache_ref, out_ref, *refs
):
    pieces, (sent_ref, taps, rows, held, sems, sem_out) = refs[: len(CHUNKS)], refs[len(CHUNKS) :]
    copies = []
    for k in range(4):
        size = 32 if k < 3 else 31
        piece = pl.ds(32 * k, size)
        copies.append(pltpu.make_async_copy(cache_ref.at[piece], held.at[piece], sems.at[k]))
        copies[-1].start()
    group = lax.broadcasted_iota(I32, (32, 512), 1) // 16
    spread = (group == lax.broadcasted_iota(I32, (32, 512), 0)).astype(F32)
    taps[0:128, :] = lax.dot_general(
        filt_ref[...], spread, (((0,), (0,)), ((), ())),
        preferred_element_type=F32, precision=HIGH,
    )
    taps[128:136, :] = jnp.zeros((8, 512), F32)
    rows[64:128, :] = jnp.zeros((64, 512), F32)
    rows[64:66, :] = taps[0:2, :]
    once = res_ref[...] * poles_ref[...]
    twice = once * poles_ref[...]
    rows[66:67, :] = jnp.sum(res_ref[...], axis=0, keepdims=True)
    rows[67:68, :] = jnp.sum(once, axis=0, keepdims=True)
    for b in range(16):
        state = state_ref[b]
        rows[32 + b : 33 + b, :] = jnp.sum(state * once, axis=0, keepdims=True)
        rows[48 + b : 49 + b, :] = jnp.sum(state * twice, axis=0, keepdims=True)
        sent_ref[b] = state.astype(BF)

    def add_tap(s, sums):
        past = held[s].astype(F32)
        return (
            sums[0] + past * taps[pl.ds(s + 1, 1), :],
            sums[1] + past * taps[pl.ds(s + 2, 1), :],
        )

    sums = (jnp.zeros((16, 512), F32),) * 2
    outs, start, size = [], 0, 0
    for k in range(4):
        copies[k].wait()
        while len(outs) < len(CHUNKS) and start + CHUNKS[len(outs)] <= 32 * k + 32:
            size = CHUNKS[len(outs)]
            outs.append(
                pltpu.make_async_copy(
                    held.at[start : start + size], pieces[len(outs)], sem_out.at[len(outs)]
                )
            )
            outs[-1].start()
            start += size
        sums = lax.fori_loop(32 * k, 32 * k + (32 if k < 3 else 31), add_tap, sums, unroll=True)
    rows[0:16, :] = sums[0]
    rows[16:32, :] = sums[1]
    columns = rows[...].T
    lane = lax.broadcasted_iota(I32, (8, 128), 1)
    start = (c_ref[1] % 4) * 32
    tok = jnp.zeros((8, 128), I32)
    for t in range(2):
        for b in range(16):
            tok = jnp.where(lane == start + 16 * t + b, tok_ref[t, b], tok)
    tok = tok.astype(F32)
    for i in range(8):
        out_ref[i, 0:64, :] = columns[64 * i : 64 * i + 64, :]
        out_ref[i, 64:72, :] = tok
    for copy in outs:
        copy.wait()


def make_sums(where, tokens, filters, poles, residues, state, cache):
    return pl.pallas_call(
        sums_kernel,
        grid=(1,),
        in_specs=[
            SMEM, SMEM, whole(32, 128), whole(16, 512), whole(16, 512), whole(16, 16, 512), HBM,
        ],
        out_specs=[whole(8, 72, 128)] + [HBM] * len(CHUNKS) + [whole(16, 16, 512)],
        out_shape=[jax.ShapeDtypeStruct((8, 72, 128), F32)]
        + [jax.ShapeDtypeStruct((size, 16, 512), BF) for size in CHUNKS + (16,)],
        scratch_shapes=[
            pltpu.VMEM((136, 512), F32),
            pltpu.VMEM((128, 512), F32),
            pltpu.VMEM((127, 16, 512), BF),
            pltpu.SemaphoreType.DMA((4,)),
            pltpu.SemaphoreType.DMA((len(CHUNKS),)),
        ],
        compiler_params=params(),
        name="state_sums",
    )(where, tokens, filters, poles, residues, state, cache)


def index_kernel(c_ref, par_ref, out_ref):
    base = c_ref[0] * 64
    lane = lax.broadcasted_iota(I32, (1, 128), 1)
    fir, onward = jnp.zeros((1, 128), I32), lane
    earlier = jnp.full((1, 128), -1, I32)
    place = lambda beam, wide: (beam >> 4) * wide + (beam & 15)
    for j in range(64):
        after = par_ref[1, base + j]
        old, older = par_ref[0, base + j] - base, par_ref[0, after] - base
        source = place(after - base, 32)
        first = lane == j // 16 * 32 + j % 16
        second = lane == j // 16 * 32 + 16 + j % 16
        fir = jnp.where(first, place(old, 128), jnp.where(second, place(older, 128) + 16, fir))
        earlier = jnp.where(second, source, earlier)
        onward = jnp.where(first, source, onward)
    out_ref[0:1, :] = fir
    out_ref[1:2, :] = fir + 32
    out_ref[2:3, :] = earlier
    out_ref[3:4, :] = onward
    out_ref[4:8, :] = jnp.zeros((4, 128), I32)


def indices(where, parents):
    return pl.pallas_call(
        index_kernel,
        grid=(1,),
        in_specs=[SMEM, SMEM],
        out_specs=whole(8, 128),
        out_shape=jax.ShapeDtypeStruct((8, 128), I32),
        compiler_params=params(),
        name="indices",
    )(where, parents)


def turn_kernel(own_ref, oth_ref, out_ref):
    for k, table in enumerate((own_ref, oth_ref)):
        out_ref[k] = table[...].T


def turn(own, oth):
    return pl.pallas_call(
        turn_kernel,
        grid=(1,),
        in_specs=[whole(512, 512)] * 2,
        out_specs=whole(2, 512, 512),
        out_shape=jax.ShapeDtypeStruct((2, 512, 512), BF),
        compiler_params=params(),
        name="turn",
    )(own, oth)


def weights(block, rows):
    return [pl.BlockSpec((1, rows // 2, 512), lambda g: (block, g, 0))] * 2


def squares_rows(x_own, x_oth):
    total = jnp.sum(x_own * x_own, axis=0, keepdims=True)
    total = total + jnp.sum(x_oth * x_oth, axis=0, keepdims=True)
    high = total.astype(BF).astype(F32)
    low = total - high
    place = lax.broadcasted_iota(I32, (EXTRA, 128), 0)
    return jnp.where(place == 0, high, jnp.where(place == 1, low, 0.0)).astype(BF)


def column(gain_ref, k):
    return jnp.broadcast_to(gain_ref[k : k + 1, :], (8, 512)).T[:, 0:1]


def hand_out(acc, rows, where_ref, outs, spread):
    half = pl.program_id(0) ^ where_ref[2]
    spread[...] = acc
    for s in range(4):
        start = pl.multiple_of(((where_ref[3] + s) & 3) * rows, rows)
        outs[s][half, 0:rows, :] = spread[pl.ds(start, rows), :]
    return half


def product_in(where_ref, w_own, w_oth, scaled, squares, spread, outs):
    acc = jnp.dot(w_own[0], scaled[0], preferred_element_type=F32)
    acc = (acc + jnp.dot(w_oth[0], scaled[1], preferred_element_type=F32)).astype(BF)
    half = hand_out(acc, 384, where_ref, outs, spread)
    for out in outs:
        out[half, 384:400, :] = squares[...]


def embed_kernel(
    c_ref, got_ref, tables, g_own, g_oth, w_own, w_oth, *refs
):
    *outs, x_ref, send_ref, scaled, squares, spread = refs

    @pl.when(pl.program_id(0) == 0)
    def _():
        c = c_ref[0]
        tok = jnp.zeros((8, 128), F32)
        for q in range(4):
            tok = tok + got_ref[c * 4 + q, 64:72, :]
            send_ref[q] = got_ref[4 - c * 4 + q, 0:64, :]
        vocab = lax.broadcasted_iota(I32, (512, 128), 0)
        onehot = (vocab == tok[0:1, :].astype(I32)).astype(BF)
        halves = []
        for k, gain in enumerate((g_own, g_oth)):
            x = jnp.dot(tables[k], onehot, preferred_element_type=F32)
            x_ref[k] = x.astype(BF)
            scaled[k] = (x * column(gain, 0)).astype(BF)
            halves.append(x)
        squares[...] = squares_rows(*halves)

    product_in(c_ref, w_own, w_oth, scaled, squares, spread, outs)


IN_SCRATCH = [
    pltpu.VMEM((2, 512, 128), BF), pltpu.VMEM((EXTRA, 128), BF), pltpu.VMEM((1536, 128), BF)
]
IN_SHAPE = [jax.ShapeDtypeStruct((2, 400, 128), BF)] * 4
IN_SPECS = [whole(2, 400, 128)] * 4
COST_IN = pl.CostEstimate(flops=2 * 3072 * 1024 * 128, bytes_accessed=7 << 20, transcendentals=0)
COST_OUT = pl.CostEstimate(flops=2 * 1024 * 1024 * 128, bytes_accessed=5 << 19, transcendentals=0)


def project_embed(where, got, tables, g_own, g_oth, w_own, w_oth):
    return pl.pallas_call(
        embed_kernel,
        grid=(2,),
        in_specs=[
            SMEM, whole(8, 72, 128), whole(2, 512, 512), whole(2, 512), whole(2, 512),
            *weights(0, 3072),
        ],
        out_specs=[*IN_SPECS, whole(2, 512, 128), whole(4, 64, 128)],
        out_shape=[
            *IN_SHAPE,
            jax.ShapeDtypeStruct((2, 512, 128), BF),
            jax.ShapeDtypeStruct((4, 64, 128), F32),
        ],
        scratch_shapes=IN_SCRATCH,
        compiler_params=params(),
        cost_estimate=COST_IN,
        name="embed_project",
    )(where, got, tables, g_own, g_oth, w_own, w_oth)


def gather_rows(c, a_ref, k):
    start = pl.multiple_of((c ^ k) * 64, 64)
    return jnp.concatenate([a_ref[i, pl.ds(start, 64), :] for i in range(8)], axis=0)


def in_kernel(c_ref, a_ref, g_own, g_oth, w_own, w_oth, *refs):
    *outs, scaled, squares, spread = refs

    @pl.when(pl.program_id(0) == 0)
    def _():
        halves = []
        for k, gain in enumerate((g_own, g_oth)):
            x = gather_rows(c_ref[0], a_ref, k).astype(F32)
            scaled[k] = (x * column(gain, 1)).astype(BF)
            halves.append(x)
        squares[...] = squares_rows(*halves)

    product_in(c_ref, w_own, w_oth, scaled, squares, spread, outs)


def project_in(where, rows, g_own, g_oth, w_own, w_oth):
    return pl.pallas_call(
        in_kernel,
        grid=(2,),
        in_specs=[
            SMEM, whole(8, 128, 128), whole(2, 512), whole(2, 512), *weights(1, 3072),
        ],
        out_specs=IN_SPECS,
        out_shape=IN_SHAPE,
        scratch_shapes=IN_SCRATCH,
        compiler_params=params(),
        cost_estimate=COST_IN,
        name="norm_project",
    )(where, rows, g_own, g_oth, w_own, w_oth)


def add_up(terms):
    *near, far = terms
    total = far[...].astype(F32)
    for term in near:
        total = total + term[0].astype(F32)
    return total


def terms_specs(rows):
    return [pl.BlockSpec((1, rows, 128), lambda g: (0, 0, 0))] * 4 + [whole(rows, 128)]


def mix_kernel(block, c_ref, *refs):
    t_own, t_oth, idx_ref, gated_ref, kv_ref = refs[5:]
    c = c_ref[0]
    total = add_up(refs[:5])
    squares = total[384:385, :] + total[385:386, :]
    feats = (total[0:384, :] * lax.rsqrt(squares / D + EPSILON)).astype(BF).astype(F32)
    kind = lambda m: jnp.concatenate(
        [feats[64 * m : 64 * m + 64, :], feats[192 + 64 * m : 256 + 64 * m, :]], axis=0
    )
    kv = (kind(1) * kind(2)).astype(BF)
    square = lax.broadcasted_iota(I32, (128, 128), 0)
    earlier = (square == idx_ref[2:3, :]).astype(BF)
    onward = (square == idx_ref[3:4, :]).astype(BF)
    kv_before = jnp.dot(kv, earlier, preferred_element_type=F32)
    kv_ref[...] = jnp.dot(kv, onward, preferred_element_type=F32).T.astype(BF)
    parts, first, second = [], [], []
    for k in range(2):
        own = c == k
        acc = jnp.zeros((64, 128), F32)
        for q in range(4):
            sums = jnp.where(own, t_own[c * 4 + q, 0:64, :], t_oth[q])
            pick = (square + 128 * q == idx_ref[block : block + 1, :]).astype(F32)
            acc = acc + jnp.dot(sums, pick, preferred_element_type=F32, precision=HIGH)
            if q == 0:
                first.append(sums[:, 64 + 2 * block : 65 + 2 * block])
                second.append(sums[:, 65 + 2 * block : 66 + 2 * block])
        parts.append(acc)
    first, second = jnp.concatenate(first, axis=0), jnp.concatenate(second, axis=0)
    filtered = first * kv.astype(F32) + second * kv_before + jnp.concatenate(parts, axis=0)
    gated = (kind(0) * filtered).astype(BF)
    for i in range(8):
        gated_ref[i] = gated


def mix(block, where, received, t_own, t_oth, idx):
    return pl.pallas_call(
        lambda *refs: mix_kernel(block, *refs),
        grid=(1,),
        in_specs=[
            SMEM, *terms_specs(400), whole(8, 72, 128), whole(4, 64, 128), whole(8, 128)
        ],
        out_specs=[whole(8, 128, 128), whole(128, 128)],
        out_shape=[
            jax.ShapeDtypeStruct((8, 128, 128), BF),
            jax.ShapeDtypeStruct((128, 128), BF),
        ],
        compiler_params=params(SMALL),
        name="mix",
    )(where, *received, t_own, t_oth, idx)


def out_kernel(c_ref, a_ref, w_own, w_oth, *refs):
    *outs, rows, spread = refs

    @pl.when(pl.program_id(0) == 0)
    def _():
        for k in range(2):
            rows[k] = gather_rows(c_ref[0], a_ref, k)

    acc = jnp.dot(w_own[0], rows[0], preferred_element_type=F32)
    acc = (acc + jnp.dot(w_oth[0], rows[1], preferred_element_type=F32)).astype(BF)
    hand_out(acc, 128, c_ref, outs, spread)


def project_out(block, where, rows, w_own, w_oth):
    return pl.pallas_call(
        out_kernel,
        grid=(2,),
        in_specs=[SMEM, whole(8, 128, 128), *weights(block, 1024)],
        out_specs=[whole(2, 128, 128)] * 4,
        out_shape=[jax.ShapeDtypeStruct((2, 128, 128), BF)] * 4,
        scratch_shapes=[pltpu.VMEM((2, 512, 128), BF), pltpu.VMEM((512, 128), BF)],
        compiler_params=params(),
        cost_estimate=COST_OUT,
        name="project_out",
    )(where, rows, w_own, w_oth)


def residual_kernel(c_ref, *refs):
    x_ref, out_ref = refs[5:]
    outward = add_up(refs[:5]).astype(BF).astype(F32)
    start = pl.multiple_of(c_ref[1] * 64, 64)
    before = jnp.concatenate(
        [x_ref[c_ref[0] ^ k, pl.ds(start, 64), :] for k in range(2)], axis=0
    )
    hidden = (before.astype(F32) + outward).astype(BF)
    for i in range(8):
        out_ref[i] = hidden


def residual(where, received, embedded):
    return pl.pallas_call(
        residual_kernel,
        grid=(1,),
        in_specs=[SMEM, *terms_specs(128), whole(2, 512, 128)],
        out_specs=whole(8, 128, 128),
        out_shape=jax.ShapeDtypeStruct((8, 128, 128), BF),
        compiler_params=params(SMALL),
        name="residual",
    )(where, *received, embedded)


def last_kernel(c_ref, *refs):
    h_ref, kv0_ref, kv1_ref, keep_ref, send_ref = refs[5:]
    outward = add_up(refs[:5]).astype(BF).astype(F32)
    hidden = (h_ref[0].astype(F32) + outward).astype(BF).astype(F32).T
    first = c_ref[0] == 0
    kv0, kv1 = kv0_ref[...].astype(F32), kv1_ref[...].astype(F32)
    pair = lambda k: jnp.concatenate(
        [hidden[:, 64 * k : 64 * k + 64], kv0[:, 64 * k : 64 * k + 64]], axis=1
    )
    low, high = pair(0), pair(1)
    keep_ref[0] = jnp.where(first, low, high).astype(BF)
    send_ref[0] = jnp.where(first, high, low).astype(BF)
    turned = pltpu.roll(kv1, 64, 1)
    keep_ref[1] = jnp.where(first, kv1, turned).astype(BF)
    send_ref[1] = jnp.where(first, turned, kv1).astype(BF)


def last(where, received, hidden, kv0, kv1):
    return pl.pallas_call(
        last_kernel,
        grid=(1,),
        in_specs=[
            SMEM, *terms_specs(128), pl.BlockSpec((1, 128, 128), lambda g: (0, 0, 0)),
            whole(128, 128), whole(128, 128),
        ],
        out_specs=[whole(2, 128, 128)] * 2,
        out_shape=[jax.ShapeDtypeStruct((2, 128, 128), BF)] * 2,
        compiler_params=params(SMALL),
        name="last",
    )(where, *received, hidden, kv0, kv1)


def arrange_kernel(c_ref, keep_ref, got_ref, out_ref):
    first = c_ref[0] == 0
    for k in range(2):
        keep, got = keep_ref[k].astype(F32), got_ref[k].astype(F32)
        for half in range(2):
            rows = jnp.where(first == (half == 0), keep, got).astype(BF)
            for q in range(4):
                out_ref[4 * half + q, 32 * k : 32 * k + 32, :] = rows[32 * q : 32 * q + 32, :]


def arrange(where, keep, got):
    return pl.pallas_call(
        arrange_kernel,
        grid=(1,),
        in_specs=[SMEM, whole(2, 128, 128), whole(2, 128, 128)],
        out_specs=whole(8, 64, 128),
        out_shape=jax.ShapeDtypeStruct((8, 64, 128), BF),
        compiler_params=params(SMALL),
        name="arrange",
    )(where, keep, got)


def origin(where_ref, par_ref, b):
    dp = where_ref[1]
    beam = par_ref[0, par_ref[1, dp * 16 + b]]
    return beam & 15, (beam >> 4) == dp


def reorder_kernel(where_ref, par_ref, own_ref, *refs):
    pieces, (out_ref, held, ready, sems, sem_out) = refs[: len(CHUNKS)], refs[len(CHUNKS) :]
    copies = [pltpu.make_async_copy(own_ref.at[0:125], held.at[0, 0:125], sems.at[0])]
    start = 0
    for k, size in enumerate(CHUNKS):
        copies.append(
            pltpu.make_async_copy(pieces[k], held.at[1, start : start + size], sems.at[k + 1])
        )
        start += size
    for copy in copies:
        copy.start()
    held[0, 125:128] = jnp.zeros((3, 16, 512), BF)
    held[1, 125:128] = jnp.zeros((3, 16, 512), BF)
    row = lax.broadcasted_iota(I32, (128, 256), 0)
    col = lax.broadcasted_iota(I32, (128, 256), 1)
    wanted = jnp.zeros((128, 256), I32)
    for b in range(16):
        slot, here = origin(where_ref, par_ref, b)
        wanted = jnp.where((row & 15) == b, slot + jnp.where(here, 0, 16), wanted)
    same_tap = ((col >> 4) & 7) == (row >> 4)
    pick = (same_tap & ((col & 15) + (col >> 7) * 16 == wanted)).astype(BF)
    for copy in copies:
        copy.wait()
    outs = []
    for k in range(16):
        taps = slice(8 * k, 8 * k + 8)
        both = jnp.concatenate(
            [held[0, taps].reshape(128, 512), held[1, taps].reshape(128, 512)], axis=0
        )
        moved = jnp.dot(pick, both, preferred_element_type=F32).astype(BF)
        ready[taps] = moved.reshape(8, 16, 512)
        size = 8 if k < 15 else 5
        outs.append(
            pltpu.make_async_copy(
                ready.at[8 * k : 8 * k + size], out_ref.at[8 * k + 2 : 8 * k + 2 + size],
                sem_out.at[k],
            )
        )
        outs[-1].start()
    for copy in outs:
        copy.wait()


def reorder(where, parents, own, pieces):
    return pl.pallas_call(
        reorder_kernel,
        in_specs=[SMEM, SMEM, HBM] + [HBM] * len(CHUNKS),
        out_specs=HBM,
        out_shape=jax.ShapeDtypeStruct((127, 16, 512), BF),
        scratch_shapes=[
            pltpu.VMEM((2, 128, 16, 512), BF),
            pltpu.VMEM((128, 16, 512), BF),
            pltpu.SemaphoreType.DMA((len(CHUNKS) + 1,)),
            pltpu.SemaphoreType.DMA((16,)),
        ],
        compiler_params=params(),
        cost_estimate=pl.CostEstimate(flops=1 << 29, bytes_accessed=6 << 20, transcendentals=0),
        name="reorder",
    )(where, parents, own, *pieces)


def final_kernel(
    where_ref, par_ref, r_ref, poles_ref, own_ref, oth_ref, fir_ref,
    hid_ref, fir_out, state_ref, fresh, sem,
):
    wide = lambda row, lane: jnp.concatenate(
        [r_ref[i, row : row + 16, :].astype(F32)[:, lane : lane + 64] for i in range(8)], axis=1
    )
    fresh[0] = wide(16, 64).astype(BF)
    fresh[1] = wide(0, 64).astype(BF)
    copy = pltpu.make_async_copy(fresh, fir_out.at[0:2], sem)
    copy.start()
    for t in range(2):
        hid_ref[t] = wide(16 * t, 0).astype(BF)
    before, now = wide(32, 0), wide(48, 0)
    poles = poles_ref[...]
    for b in range(16):
        slot, here = origin(where_ref, par_ref, b)
        old = jnp.where(here, own_ref[slot], oth_ref[slot].astype(F32))
        state_ref[b] = poles * (poles * old + before[b : b + 1, :]) + now[b : b + 1, :]
    copy.wait()


def final(where, parents, received, poles, own, oth, fir):
    return pl.pallas_call(
        final_kernel,
        grid=(1,),
        in_specs=[
            SMEM, SMEM, whole(8, 64, 128), whole(16, 512), whole(16, 16, 512),
            whole(16, 16, 512), HBM,
        ],
        out_specs=[whole(2, 16, 512), HBM, whole(16, 16, 512)],
        out_shape=[
            jax.ShapeDtypeStruct((2, 16, 512), BF),
            jax.ShapeDtypeStruct((127, 16, 512), BF),
            jax.ShapeDtypeStruct((16, 16, 512), F32),
        ],
        scratch_shapes=[pltpu.VMEM((2, 16, 512), BF), pltpu.SemaphoreType.DMA],
        input_output_aliases={6: 1},
        compiler_params=params(),
        name="final",
    )(where, parents, received, poles, own, oth, fir)


def local(
    tokens, parents, embed_table, norm_gain, weight_in, weight_out, fir_filters, mode_poles,
    residues, fir_cache, modal_state,
):
    dp = lax.axis_index(DP).astype(I32)
    c = lax.axis_index("c").astype(I32)
    where = jnp.stack([c, dp, lax.axis_index("xh").astype(I32), lax.axis_index("z").astype(I32)])
    w_in = weight_in.reshape(2, 3072, 512)
    w_out = weight_out.reshape(2, 1024, 512)
    cache = jnp.transpose(fir_cache, (1, 0, 2))
    e_oth = swap(embed_table, "c")
    g_oth = swap(norm_gain, "c")
    sums, *pieces = make_sums(
        where, tokens, fir_filters, mode_poles, residues, modal_state, cache
    )
    w_in, w_out, e_oth, g_oth, sums = lax.optimization_barrier(
        (w_in, w_out, e_oth, g_oth, sums)
    )
    w_in_oth = swap(w_in, "c")
    w_out_oth = swap(w_out, "c")
    moved = []

    def send(trigger):
        piece, trigger, moved[-1:] = lax.optimization_barrier(
            (pieces[len(moved)], trigger, moved[-1:])
        )
        moved.append(swap(piece, "xl"))
        return trigger

    def scatter(terms):
        terms = list(terms)
        for s in (2, 1, 3):
            terms[s] = lax.ppermute(terms[s], "z", [(z, (z + s) % 4) for z in range(4)])
        far = sum(term[1].astype(F32) for term in terms).astype(BF)
        far, moved[-1] = lax.optimization_barrier((far, moved[-1]))
        return *terms, swap(far, "xh")

    idx = indices(where, parents)
    tables = turn(embed_table, e_oth)
    got, idx, tables = lax.optimization_barrier((exchange(sums, DP), idx, tables))
    *partial, embedded, t_send = project_embed(
        where, send(got), tables, norm_gain, g_oth, w_in, w_in_oth
    )
    t_oth = swap(t_send, "c")
    gated, kv0 = mix(0, where, scatter(partial), got, t_oth, idx)
    partial = project_out(
        0, where, send(exchange(gated, DP)), w_out, w_out_oth
    )
    hidden = residual(where, scatter(partial), embedded)
    partial = project_in(
        where, send(exchange(hidden, DP)), norm_gain, g_oth, w_in, w_in_oth
    )
    gated, kv1 = mix(1, where, scatter(partial), got, t_oth, idx)
    partial = project_out(
        1, where, send(exchange(gated, DP)), w_out, w_out_oth
    )
    keep, crossing = last(where, scatter(partial), hidden, kv0, kv1)
    received = exchange(arrange(where, keep, swap(crossing, "c")), DP)
    *moved, state_oth = moved
    fir_before = reorder(where, parents, cache, moved)
    hidden_out, fir_next, state_next = final(
        where, parents, received, mode_poles, modal_state, state_oth, fir_before
    )
    return hidden_out, jnp.transpose(fir_next, (1, 0, 2)), state_next


def solution(mesh):
    fine = Mesh(mesh.devices.reshape(4, 2, 2, 4, 2), ("y", "xl", "xh", "z", "c"))
    return jax.shard_map(
        local,
        mesh=fine,
        in_specs=(
            P(None, DP),
            P(),
            P(None, CHAN),
            P(None, CHAN),
            P(None, None, DP, None, None, CHAN),
            P(None, None, DP, None, CHAN),
            P(CHAN, None),
            P(None, CHAN),
            P(None, CHAN),
            P(DP, None, CHAN),
            P(DP, None, CHAN),
        ),
        out_specs=(P(None, DP, CHAN), P(DP, None, CHAN), P(DP, None, CHAN)),
        check_vma=False,
    )
```

```python
import jax
import jax.numpy as jnp
from jax import lax
from jax.experimental import pallas as pl
from jax.experimental.pallas import tpu as pltpu
from jax.sharding import Mesh, PartitionSpec as P

D = 8192
EPSILON = 1e-05
BF = jnp.bfloat16
F32 = jnp.float32
I32 = jnp.int32
HIGH = lax.Precision.HIGHEST
DP = ("y", "xl")
CHAN = ("xh", "z", "c")
XZ = ("xh", "z")
SMEM = pl.BlockSpec(memory_space=pltpu.SMEM)
HBM = pl.BlockSpec(memory_space=pltpu.HBM)
LARGE = 62 * 1024 * 1024 + 512 * 1024
SMALL = 8 * 1024 * 1024
CHUNKS = (57, 22, 46)
EXTRA = 16


def params(limit=LARGE):
    return pltpu.CompilerParams(vmem_limit_bytes=limit)


def whole(*shape):
    return pl.BlockSpec(shape, lambda g: (0,) * len(shape))


def swap(value, axis):
    return lax.ppermute(value, axis, [(0, 1), (1, 0)])


def exchange(value, axes):
    return lax.all_to_all(value, axes, 0, 0, tiled=True)


def sums_kernel(
    tok_ref, filt_ref, poles_ref, res_ref, state_ref, cache_ref, out_ref, *refs
):
    pieces, (sent_ref, taps, rows, held, sems, sem_out) = refs[: len(CHUNKS)], refs[len(CHUNKS) :]
    copies = []
    for k in range(4):
        size = 32 if k < 3 else 31
        piece = pl.ds(32 * k, size)
        copies.append(pltpu.make_async_copy(cache_ref.at[piece], held.at[piece], sems.at[k]))
        copies[-1].start()
    group = lax.broadcasted_iota(I32, (32, 512), 1) // 16
    spread = (group == lax.broadcasted_iota(I32, (32, 512), 0)).astype(F32)
    taps[0:128, :] = lax.dot_general(
        filt_ref[...], spread, (((0,), (0,)), ((), ())),
        preferred_element_type=F32, precision=HIGH,
    )
    taps[128:136, :] = jnp.zeros((8, 512), F32)
    rows[64:128, :] = jnp.zeros((64, 512), F32)
    once = res_ref[...] * poles_ref[...]
    twice = once * poles_ref[...]
    gains = (
        taps[0:1, :], taps[1:2, :],
        jnp.sum(res_ref[...], axis=0, keepdims=True), jnp.sum(once, axis=0, keepdims=True),
    )
    for k, gain in enumerate(gains):
        high = gain.astype(BF).astype(F32)
        rows[64 + k : 65 + k, :] = high
        rows[72 + k : 73 + k, :] = gain - high
    for b in range(16):
        state = state_ref[b]
        rows[32 + b : 33 + b, :] = jnp.sum(state * once, axis=0, keepdims=True)
        rows[48 + b : 49 + b, :] = jnp.sum(state * twice, axis=0, keepdims=True)
        sent_ref[b] = state.astype(BF)

    def add_tap(s, sums):
        past = held[s].astype(F32)
        return (
            sums[0] + past * taps[pl.ds(s + 1, 1), :],
            sums[1] + past * taps[pl.ds(s + 2, 1), :],
        )

    sums = (jnp.zeros((16, 512), F32),) * 2
    outs, start, size = [], 0, 0
    for k in range(4):
        copies[k].wait()
        while len(outs) < len(CHUNKS) and start + CHUNKS[len(outs)] <= 32 * k + 32:
            size = CHUNKS[len(outs)]
            outs.append(
                pltpu.make_async_copy(
                    held.at[start : start + size], pieces[len(outs)], sem_out.at[len(outs)]
                )
            )
            outs[-1].start()
            start += size
        sums = lax.fori_loop(32 * k, 32 * k + (32 if k < 3 else 31), add_tap, sums, unroll=True)
    rows[0:16, :] = sums[0]
    rows[16:32, :] = sums[1]
    columns = rows[...].T
    columns = columns.astype(BF)
    lane = lax.broadcasted_iota(I32, (16, 128), 1)
    start = ((lax.axis_index("y") & 1) * 2 + lax.axis_index("xl")) * 32
    tok = jnp.zeros((16, 128), I32)
    for t in range(2):
        for b in range(16):
            tok = jnp.where(lane == start + 16 * t + b, tok_ref[t, b], tok)
    first = lax.broadcasted_iota(I32, (16, 128), 0) == 0
    tok = jnp.where(first, tok >> 4, tok & 15).astype(F32).astype(BF)
    for i in range(8):
        out_ref[i, 0:64, :] = columns[64 * i : 64 * i + 64, :]
        out_ref[i, 64:80, :] = tok
    for copy in outs:
        copy.wait()


def make_sums(tokens, filters, poles, residues, state, cache):
    return pl.pallas_call(
        sums_kernel,
        grid=(1,),
        in_specs=[
            SMEM, whole(32, 128), whole(16, 512), whole(16, 512), whole(16, 16, 512), HBM,
        ],
        out_specs=[whole(8, 80, 128)] + [HBM] * len(CHUNKS) + [whole(16, 16, 512)],
        out_shape=[jax.ShapeDtypeStruct((8, 80, 128), BF)]
        + [jax.ShapeDtypeStruct((size, 16, 512), BF) for size in CHUNKS + (16,)],
        scratch_shapes=[
            pltpu.VMEM((136, 512), F32),
            pltpu.VMEM((128, 512), F32),
            pltpu.VMEM((127, 16, 512), BF),
            pltpu.SemaphoreType.DMA((4,)),
            pltpu.SemaphoreType.DMA((len(CHUNKS),)),
        ],
        compiler_params=params(),
        name="state_sums",
    )(tokens, filters, poles, residues, state, cache)


def index_kernel(c_ref, par_ref, out_ref):
    base = c_ref[0] * 64
    lane = lax.broadcasted_iota(I32, (1, 128), 1)
    fir, onward = jnp.zeros((1, 128), I32), lane
    earlier = jnp.full((1, 128), -1, I32)
    place = lambda beam, wide: (beam >> 4) * wide + (beam & 15)
    for j in range(64):
        after = par_ref[1, base + j]
        old, older = par_ref[0, base + j] - base, par_ref[0, after] - base
        source = place(after - base, 32)
        first = lane == j // 16 * 32 + j % 16
        second = lane == j // 16 * 32 + 16 + j % 16
        fir = jnp.where(first, place(old, 128), jnp.where(second, place(older, 128) + 16, fir))
        earlier = jnp.where(second, source, earlier)
        onward = jnp.where(first, source, onward)
    out_ref[0:1, :] = fir
    out_ref[1:2, :] = fir + 32
    out_ref[2:3, :] = earlier
    out_ref[3:4, :] = onward
    out_ref[4:8, :] = jnp.zeros((4, 128), I32)


def indices(where, parents):
    return pl.pallas_call(
        index_kernel,
        grid=(1,),
        in_specs=[SMEM, SMEM],
        out_specs=whole(8, 128),
        out_shape=jax.ShapeDtypeStruct((8, 128), I32),
        compiler_params=params(),
        name="indices",
    )(where, parents)


def turn_kernel(own_ref, oth_ref, out_ref):
    for k, table in enumerate((own_ref, oth_ref)):
        out_ref[k] = table[...].T


def turn(own, oth):
    return pl.pallas_call(
        turn_kernel,
        grid=(1,),
        in_specs=[whole(512, 512)] * 2,
        out_specs=whole(2, 512, 512),
        out_shape=jax.ShapeDtypeStruct((2, 512, 512), BF),
        compiler_params=params(),
        name="turn",
    )(own, oth)


def weights(block, rows):
    return [pl.BlockSpec((1, rows // 2, 512), lambda g: (block, g, 0))] * 2


def squares_rows(x_own, x_oth):
    total = jnp.sum(x_own * x_own, axis=0, keepdims=True)
    total = total + jnp.sum(x_oth * x_oth, axis=0, keepdims=True)
    high = total.astype(BF).astype(F32)
    low = total - high
    place = lax.broadcasted_iota(I32, (EXTRA, 128), 0)
    return jnp.where(place == 0, high, jnp.where(place == 1, low, 0.0)).astype(BF)


def column(gain_ref, k):
    return jnp.broadcast_to(gain_ref[k : k + 1, :], (8, 512)).T[:, 0:1]


def hand_out(acc, rows, where_ref, outs, spread):
    half = pl.program_id(0) ^ where_ref[2]
    spread[...] = acc
    for s in range(4):
        start = pl.multiple_of(((where_ref[3] + s) & 3) * rows, rows)
        outs[s][half, 0:rows, :] = spread[pl.ds(start, rows), :]
    return half


def product_in(where_ref, w_own, w_oth, scaled, squares, spread, outs):
    acc = jnp.dot(w_own[0], scaled[0], preferred_element_type=F32)
    acc = (acc + jnp.dot(w_oth[0], scaled[1], preferred_element_type=F32)).astype(BF)
    half = hand_out(acc, 384, where_ref, outs, spread)
    for out in outs:
        out[half, 384:400, :] = squares[...]


def embed_kernel(
    c_ref, got_ref, tables, g_own, g_oth, w_own, w_oth, *refs
):
    *outs, x_ref, send_ref, scaled, squares, spread = refs

    @pl.when(pl.program_id(0) == 0)
    def _():
        c = c_ref[0]
        tok = jnp.zeros((16, 128), F32)
        for q in range(4):
            tok = tok + got_ref[c * 4 + q, 64:80, :].astype(F32)
            send_ref[q] = got_ref[4 - c * 4 + q, 0:64, :]
        vocab = lax.broadcasted_iota(I32, (512, 128), 0)
        tok = (tok[0:1, :] * 16.0 + tok[1:2, :] + 0.5).astype(I32)
        onehot = (vocab == tok).astype(BF)
        halves = []
        for k, gain in enumerate((g_own, g_oth)):
            x = jnp.dot(tables[k], onehot, preferred_element_type=F32)
            x_ref[k] = x.astype(BF)
            scaled[k] = (x * column(gain, 0)).astype(BF)
            halves.append(x)
        squares[...] = squares_rows(*halves)

    product_in(c_ref, w_own, w_oth, scaled, squares, spread, outs)


IN_SCRATCH = [
    pltpu.VMEM((2, 512, 128), BF), pltpu.VMEM((EXTRA, 128), BF), pltpu.VMEM((1536, 128), BF)
]
IN_SHAPE = [jax.ShapeDtypeStruct((2, 400, 128), BF)] * 4
IN_SPECS = [whole(2, 400, 128)] * 4
COST_IN = pl.CostEstimate(flops=2 * 3072 * 1024 * 128, bytes_accessed=7 << 20, transcendentals=0)
COST_OUT = pl.CostEstimate(flops=2 * 1024 * 1024 * 128, bytes_accessed=5 << 19, transcendentals=0)


def project_embed(where, got, tables, g_own, g_oth, w_own, w_oth):
    return pl.pallas_call(
        embed_kernel,
        grid=(2,),
        in_specs=[
            SMEM, whole(8, 80, 128), whole(2, 512, 512), whole(2, 512), whole(2, 512),
            *weights(0, 3072),
        ],
        out_specs=[*IN_SPECS, whole(2, 512, 128), whole(4, 64, 128)],
        out_shape=[
            *IN_SHAPE,
            jax.ShapeDtypeStruct((2, 512, 128), BF),
            jax.ShapeDtypeStruct((4, 64, 128), BF),
        ],
        scratch_shapes=IN_SCRATCH,
        compiler_params=params(),
        cost_estimate=COST_IN,
        name="embed_project",
    )(where, got, tables, g_own, g_oth, w_own, w_oth)


def gather_rows(c, a_ref, k):
    start = pl.multiple_of((c ^ k) * 64, 64)
    return jnp.concatenate([a_ref[i, pl.ds(start, 64), :] for i in range(8)], axis=0)


def in_kernel(c_ref, a_ref, g_own, g_oth, w_own, w_oth, *refs):
    *outs, scaled, squares, spread = refs

    @pl.when(pl.program_id(0) == 0)
    def _():
        halves = []
        for k, gain in enumerate((g_own, g_oth)):
            x = gather_rows(c_ref[0], a_ref, k).astype(F32)
            scaled[k] = (x * column(gain, 1)).astype(BF)
            halves.append(x)
        squares[...] = squares_rows(*halves)

    product_in(c_ref, w_own, w_oth, scaled, squares, spread, outs)


def project_in(where, rows, g_own, g_oth, w_own, w_oth):
    return pl.pallas_call(
        in_kernel,
        grid=(2,),
        in_specs=[
            SMEM, whole(8, 128, 128), whole(2, 512), whole(2, 512), *weights(1, 3072),
        ],
        out_specs=IN_SPECS,
        out_shape=IN_SHAPE,
        scratch_shapes=IN_SCRATCH,
        compiler_params=params(),
        cost_estimate=COST_IN,
        name="norm_project",
    )(where, rows, g_own, g_oth, w_own, w_oth)


def add_up(terms):
    *near, far = terms
    total = far[...].astype(F32)
    for term in near:
        total = total + term[0].astype(F32)
    return total


def terms_specs(rows):
    return [pl.BlockSpec((1, rows, 128), lambda g: (0, 0, 0))] * 4 + [whole(rows, 128)]


def mix_kernel(block, c_ref, *refs):
    t_own, t_oth, idx_ref, gated_ref, kv_ref = refs[5:]
    c = c_ref[0]
    total = add_up(refs[:5])
    squares = total[384:385, :] + total[385:386, :]
    feats = (total[0:384, :] * lax.rsqrt(squares / D + EPSILON)).astype(BF).astype(F32)
    kind = lambda m: jnp.concatenate(
        [feats[64 * m : 64 * m + 64, :], feats[192 + 64 * m : 256 + 64 * m, :]], axis=0
    )
    kv = (kind(1) * kind(2)).astype(BF)
    square = lax.broadcasted_iota(I32, (128, 128), 0)
    earlier = (square == idx_ref[2:3, :]).astype(BF)
    onward = (square == idx_ref[3:4, :]).astype(BF)
    kv_before = jnp.dot(kv, earlier, preferred_element_type=F32)
    kv_ref[...] = jnp.dot(kv, onward, preferred_element_type=F32).T.astype(BF)
    parts, first, second = [], [], []
    for k in range(2):
        own = c == k
        acc = jnp.zeros((64, 128), F32)
        for q in range(4):
            sums = jnp.where(own, t_own[c * 4 + q, 0:64, :].astype(F32), t_oth[q].astype(F32))
            pick = (square + 128 * q == idx_ref[block : block + 1, :]).astype(BF)
            acc = acc + jnp.dot(sums.astype(BF), pick, preferred_element_type=F32)
            if q == 0:
                gain = lambda lane: sums[:, lane : lane + 1] + sums[:, lane + 8 : lane + 9]
                first.append(gain(64 + 2 * block))
                second.append(gain(65 + 2 * block))
        parts.append(acc)
    first, second = jnp.concatenate(first, axis=0), jnp.concatenate(second, axis=0)
    filtered = first * kv.astype(F32) + second * kv_before + jnp.concatenate(parts, axis=0)
    gated = (kind(0) * filtered).astype(BF)
    for i in range(8):
        gated_ref[i] = gated


def mix(block, where, received, t_own, t_oth, idx):
    return pl.pallas_call(
        lambda *refs: mix_kernel(block, *refs),
        grid=(1,),
        in_specs=[
            SMEM, *terms_specs(400), whole(8, 80, 128), whole(4, 64, 128), whole(8, 128)
        ],
        out_specs=[whole(8, 128, 128), whole(128, 128)],
        out_shape=[
            jax.ShapeDtypeStruct((8, 128, 128), BF),
            jax.ShapeDtypeStruct((128, 128), BF),
        ],
        compiler_params=params(SMALL),
        name="mix",
    )(where, *received, t_own, t_oth, idx)


def out_kernel(c_ref, a_ref, w_own, w_oth, out_ref, rows):

    @pl.when(pl.program_id(0) == 0)
    def _():
        for k in range(2):
            rows[k] = gather_rows(c_ref[0], a_ref, k)

    acc = jnp.dot(w_own[0], rows[0], preferred_element_type=F32)
    acc = (acc + jnp.dot(w_oth[0], rows[1], preferred_element_type=F32)).astype(BF)
    for k in range(4):
        out_ref[k] = acc[128 * k : 128 * k + 128, :]


def project_out(block, where, rows, w_own, w_oth):
    return pl.pallas_call(
        out_kernel,
        grid=(2,),
        in_specs=[SMEM, whole(8, 128, 128), *weights(block, 1024)],
        out_specs=pl.BlockSpec((4, 128, 128), lambda g: (g, 0, 0)),
        out_shape=jax.ShapeDtypeStruct((8, 128, 128), BF),
        scratch_shapes=[pltpu.VMEM((2, 512, 128), BF)],
        compiler_params=params(),
        cost_estimate=COST_OUT,
        name="project_out",
    )(where, rows, w_own, w_oth)


def add_blocks(r_ref):
    total = r_ref[0].astype(F32)
    for g in range(1, 8):
        total = total + r_ref[g].astype(F32)
    return total.astype(BF).astype(F32)


def residual_kernel(c_ref, r_ref, x_ref, out_ref):
    outward = add_blocks(r_ref)
    start = pl.multiple_of(c_ref[1] * 64, 64)
    before = jnp.concatenate(
        [x_ref[c_ref[0] ^ k, pl.ds(start, 64), :] for k in range(2)], axis=0
    )
    hidden = (before.astype(F32) + outward).astype(BF)
    for i in range(8):
        out_ref[i] = hidden


def residual(where, received, embedded):
    return pl.pallas_call(
        residual_kernel,
        grid=(1,),
        in_specs=[SMEM, whole(8, 128, 128), whole(2, 512, 128)],
        out_specs=whole(8, 128, 128),
        out_shape=jax.ShapeDtypeStruct((8, 128, 128), BF),
        compiler_params=params(SMALL),
        name="residual",
    )(where, received, embedded)


def last_kernel(c_ref, r_ref, h_ref, kv0_ref, kv1_ref, keep_ref, send_ref):
    outward = add_blocks(r_ref)
    hidden = (h_ref[0].astype(F32) + outward).astype(BF).astype(F32).T
    first = c_ref[0] == 0
    kv0, kv1 = kv0_ref[...].astype(F32), kv1_ref[...].astype(F32)
    pair = lambda k: jnp.concatenate(
        [hidden[:, 64 * k : 64 * k + 64], kv0[:, 64 * k : 64 * k + 64]], axis=1
    )
    low, high = pair(0), pair(1)
    keep_ref[0] = jnp.where(first, low, high).astype(BF)
    send_ref[0] = jnp.where(first, high, low).astype(BF)
    turned = pltpu.roll(kv1, 64, 1)
    keep_ref[1] = jnp.where(first, kv1, turned).astype(BF)
    send_ref[1] = jnp.where(first, turned, kv1).astype(BF)


def last(where, received, hidden, kv0, kv1):
    return pl.pallas_call(
        last_kernel,
        grid=(1,),
        in_specs=[
            SMEM, whole(8, 128, 128), pl.BlockSpec((1, 128, 128), lambda g: (0, 0, 0)),
            whole(128, 128), whole(128, 128),
        ],
        out_specs=[whole(2, 128, 128)] * 2,
        out_shape=[jax.ShapeDtypeStruct((2, 128, 128), BF)] * 2,
        compiler_params=params(SMALL),
        name="last",
    )(where, received, hidden, kv0, kv1)


def arrange_kernel(c_ref, keep_ref, got_ref, out_ref):
    first = c_ref[0] == 0
    for k in range(2):
        keep, got = keep_ref[k].astype(F32), got_ref[k].astype(F32)
        for half in range(2):
            rows = jnp.where(first == (half == 0), keep, got).astype(BF)
            for q in range(4):
                out_ref[4 * half + q, 32 * k : 32 * k + 32, :] = rows[32 * q : 32 * q + 32, :]


def arrange(where, keep, got):
    return pl.pallas_call(
        arrange_kernel,
        grid=(1,),
        in_specs=[SMEM, whole(2, 128, 128), whole(2, 128, 128)],
        out_specs=whole(8, 64, 128),
        out_shape=jax.ShapeDtypeStruct((8, 64, 128), BF),
        compiler_params=params(SMALL),
        name="arrange",
    )(where, keep, got)


def origin(where_ref, par_ref, b):
    dp = where_ref[1]
    beam = par_ref[0, par_ref[1, dp * 16 + b]]
    return beam & 15, (beam >> 4) == dp


def reorder_kernel(where_ref, par_ref, own_ref, *refs):
    pieces, (out_ref, held, ready, sems, sem_out) = refs[: len(CHUNKS)], refs[len(CHUNKS) :]
    copies = [pltpu.make_async_copy(own_ref.at[0:125], held.at[0, 0:125], sems.at[0])]
    start = 0
    for k, size in enumerate(CHUNKS):
        copies.append(
            pltpu.make_async_copy(pieces[k], held.at[1, start : start + size], sems.at[k + 1])
        )
        start += size
    for copy in copies:
        copy.start()
    held[0, 125:128] = jnp.zeros((3, 16, 512), BF)
    held[1, 125:128] = jnp.zeros((3, 16, 512), BF)
    row = lax.broadcasted_iota(I32, (128, 256), 0)
    col = lax.broadcasted_iota(I32, (128, 256), 1)
    wanted = jnp.zeros((128, 256), I32)
    for b in range(16):
        slot, here = origin(where_ref, par_ref, b)
        wanted = jnp.where((row & 15) == b, slot + jnp.where(here, 0, 16), wanted)
    same_tap = ((col >> 4) & 7) == (row >> 4)
    pick = (same_tap & ((col & 15) + (col >> 7) * 16 == wanted)).astype(BF)
    for copy in copies:
        copy.wait()
    outs = []
    for k in range(16):
        taps = slice(8 * k, 8 * k + 8)
        both = jnp.concatenate(
            [held[0, taps].reshape(128, 512), held[1, taps].reshape(128, 512)], axis=0
        )
        moved = jnp.dot(pick, both, preferred_element_type=F32).astype(BF)
        ready[taps] = moved.reshape(8, 16, 512)
        size = 8 if k < 15 else 5
        outs.append(
            pltpu.make_async_copy(
                ready.at[8 * k : 8 * k + size], out_ref.at[8 * k + 2 : 8 * k + 2 + size],
                sem_out.at[k],
            )
        )
        outs[-1].start()
    for copy in outs:
        copy.wait()


def reorder(where, parents, own, pieces):
    return pl.pallas_call(
        reorder_kernel,
        in_specs=[SMEM, SMEM, HBM] + [HBM] * len(CHUNKS),
        out_specs=HBM,
        out_shape=jax.ShapeDtypeStruct((127, 16, 512), BF),
        scratch_shapes=[
            pltpu.VMEM((2, 128, 16, 512), BF),
            pltpu.VMEM((128, 16, 512), BF),
            pltpu.SemaphoreType.DMA((len(CHUNKS) + 1,)),
            pltpu.SemaphoreType.DMA((16,)),
        ],
        compiler_params=params(),
        cost_estimate=pl.CostEstimate(flops=1 << 29, bytes_accessed=6 << 20, transcendentals=0),
        name="reorder",
    )(where, parents, own, *pieces)


def final_kernel(
    where_ref, par_ref, r_ref, poles_ref, own_ref, oth_ref, fir_ref,
    hid_ref, fir_out, state_ref, fresh, sem,
):
    wide = lambda row, lane: jnp.concatenate(
        [r_ref[i, row : row + 16, :].astype(F32)[:, lane : lane + 64] for i in range(8)], axis=1
    )
    fresh[0] = wide(16, 64).astype(BF)
    fresh[1] = wide(0, 64).astype(BF)
    copy = pltpu.make_async_copy(fresh, fir_out.at[0:2], sem)
    copy.start()
    for t in range(2):
        hid_ref[t] = wide(16 * t, 0).astype(BF)
    before, now = wide(32, 0), wide(48, 0)
    poles = poles_ref[...]
    for b in range(16):
        slot, here = origin(where_ref, par_ref, b)
        old = jnp.where(here, own_ref[slot], oth_ref[slot].astype(F32))
        state_ref[b] = poles * (poles * old + before[b : b + 1, :]) + now[b : b + 1, :]
    copy.wait()


def final(where, parents, received, poles, own, oth, fir):
    return pl.pallas_call(
        final_kernel,
        grid=(1,),
        in_specs=[
            SMEM, SMEM, whole(8, 64, 128), whole(16, 512), whole(16, 16, 512),
            whole(16, 16, 512), HBM,
        ],
        out_specs=[whole(2, 16, 512), HBM, whole(16, 16, 512)],
        out_shape=[
            jax.ShapeDtypeStruct((2, 16, 512), BF),
            jax.ShapeDtypeStruct((127, 16, 512), BF),
            jax.ShapeDtypeStruct((16, 16, 512), F32),
        ],
        scratch_shapes=[pltpu.VMEM((2, 16, 512), BF), pltpu.SemaphoreType.DMA],
        input_output_aliases={6: 1},
        compiler_params=params(),
        name="final",
    )(where, parents, received, poles, own, oth, fir)


def local(
    tokens, parents, embed_table, norm_gain, weight_in, weight_out, fir_filters, mode_poles,
    residues, fir_cache, modal_state,
):
    dp = lax.axis_index(DP).astype(I32)
    c = lax.axis_index("c").astype(I32)
    where = jnp.stack([c, dp, lax.axis_index("xh").astype(I32), lax.axis_index("z").astype(I32)])
    w_in = weight_in.reshape(2, 3072, 512)
    w_out = weight_out.reshape(2, 1024, 512)
    cache = jnp.transpose(fir_cache, (1, 0, 2))
    e_oth = swap(embed_table, "c")
    g_oth = swap(norm_gain, "c")
    sums, *pieces = make_sums(
        tokens, fir_filters, mode_poles, residues, modal_state, cache
    )
    w_in, w_out, e_oth, g_oth, sums = lax.optimization_barrier(
        (w_in, w_out, e_oth, g_oth, sums)
    )
    w_in_oth = swap(w_in, "c")
    w_out_oth = swap(w_out, "c")
    moved = []

    def send(trigger):
        piece, trigger, moved[-1:] = lax.optimization_barrier(
            (pieces[len(moved)], trigger, moved[-1:])
        )
        moved.append(swap(piece, "xl"))
        return trigger

    def scatter(terms):
        terms = list(terms)
        for s in (2, 1, 3):
            terms[s] = lax.ppermute(terms[s], "z", [(z, (z + s) % 4) for z in range(4)])
        far = sum(term[1].astype(F32) for term in terms).astype(BF)
        far, moved[-1] = lax.optimization_barrier((far, moved[-1]))
        return *terms, swap(far, "xh")

    idx = indices(where, parents)
    tables = turn(embed_table, e_oth)
    got, idx, tables = lax.optimization_barrier((exchange(sums, DP), idx, tables))
    *partial, embedded, t_send = project_embed(
        where, send(got), tables, norm_gain, g_oth, w_in, w_in_oth
    )
    t_oth = swap(t_send, "c")
    def gather(rows):
        rows, moved[-1] = lax.optimization_barrier((exchange(send(rows), DP), moved[-1]))
        return rows

    gated, kv0 = mix(0, where, scatter(partial), got, t_oth, idx)
    partial = project_out(0, where, gather(gated), w_out, w_out_oth)
    hidden = residual(where, exchange(partial, XZ), embedded)
    rows = send(exchange(hidden, DP))
    partial = project_in(where, rows, norm_gain, g_oth, w_in, w_in_oth)
    gated, kv1 = mix(1, where, scatter(partial), got, t_oth, idx)
    partial = project_out(1, where, gather(gated), w_out, w_out_oth)
    keep, crossing = last(where, exchange(partial, XZ), hidden, kv0, kv1)
    received = exchange(arrange(where, keep, swap(crossing, "c")), DP)
    *moved, state_oth = moved
    fir_before = reorder(where, parents, cache, moved)
    hidden_out, fir_next, state_next = final(
        where, parents, received, mode_poles, modal_state, state_oth, fir_before
    )
    return hidden_out, jnp.transpose(fir_next, (1, 0, 2)), state_next


def solution(mesh):
    fine = Mesh(mesh.devices.reshape(4, 2, 2, 4, 2), ("y", "xl", "xh", "z", "c"))
    return jax.shard_map(
        local,
        mesh=fine,
        in_specs=(
            P(None, DP),
            P(),
            P(None, CHAN),
            P(None, CHAN),
            P(None, None, DP, None, None, CHAN),
            P(None, None, DP, None, CHAN),
            P(CHAN, None),
            P(None, CHAN),
            P(None, CHAN),
            P(DP, None, CHAN),
            P(DP, None, CHAN),
        ),
        out_specs=(P(None, DP, CHAN), P(DP, None, CHAN), P(DP, None, CHAN)),
        check_vma=False,
    )
```

```python
import jax
import jax.numpy as jnp
from jax import lax
from jax.experimental import pallas as pl
from jax.experimental.pallas import tpu as pltpu
from jax.sharding import Mesh, PartitionSpec as P

D = 8192
EPSILON = 1e-05
BF = jnp.bfloat16
F32 = jnp.float32
I32 = jnp.int32
HIGH = lax.Precision.HIGHEST
DP = ("y", "xl")
CHAN = ("xh", "z", "c")
XZ = ("xh", "z")
SMEM = pl.BlockSpec(memory_space=pltpu.SMEM)
HBM = pl.BlockSpec(memory_space=pltpu.HBM)
LARGE = 62 * 1024 * 1024 + 512 * 1024
SMALL = 8 * 1024 * 1024
CHUNKS = (57, 22, 46)
EXTRA = 16


def params(limit=LARGE):
    return pltpu.CompilerParams(vmem_limit_bytes=limit)


def whole(*shape):
    return pl.BlockSpec(shape, lambda g: (0,) * len(shape))


def swap(value, axis):
    return lax.ppermute(value, axis, [(0, 1), (1, 0)])


def exchange(value, axes):
    return lax.all_to_all(value, axes, 0, 0, tiled=True)


def sums_kernel(
    tok_ref, filt_ref, poles_ref, res_ref, state_ref, cache_ref, out_ref, *refs
):
    pieces, (sent_ref, taps, rows, held, sems, sem_out) = refs[: len(CHUNKS)], refs[len(CHUNKS) :]
    copies = []
    for k in range(4):
        size = 32 if k < 3 else 31
        piece = pl.ds(32 * k, size)
        copies.append(pltpu.make_async_copy(cache_ref.at[piece], held.at[piece], sems.at[k]))
        copies[-1].start()
    group = lax.broadcasted_iota(I32, (32, 512), 1) // 16
    spread = (group == lax.broadcasted_iota(I32, (32, 512), 0)).astype(F32)
    taps[0:128, :] = lax.dot_general(
        filt_ref[...], spread, (((0,), (0,)), ((), ())),
        preferred_element_type=F32, precision=HIGH,
    )
    taps[128:136, :] = jnp.zeros((8, 512), F32)
    rows[64:128, :] = jnp.zeros((64, 512), F32)
    once = res_ref[...] * poles_ref[...]
    twice = once * poles_ref[...]
    gains = (
        taps[0:1, :], taps[1:2, :],
        jnp.sum(res_ref[...], axis=0, keepdims=True), jnp.sum(once, axis=0, keepdims=True),
    )
    for k, gain in enumerate(gains):
        high = gain.astype(BF).astype(F32)
        rows[64 + k : 65 + k, :] = high
        rows[72 + k : 73 + k, :] = gain - high
    for b in range(16):
        state = state_ref[b]
        rows[32 + b : 33 + b, :] = jnp.sum(state * once, axis=0, keepdims=True)
        rows[48 + b : 49 + b, :] = jnp.sum(state * twice, axis=0, keepdims=True)
        sent_ref[b] = state.astype(BF)

    def add_tap(s, sums):
        past = held[s].astype(F32)
        return (
            sums[0] + past * taps[pl.ds(s + 1, 1), :],
            sums[1] + past * taps[pl.ds(s + 2, 1), :],
        )

    sums = (jnp.zeros((16, 512), F32),) * 2
    outs, start, size = [], 0, 0
    for k in range(4):
        copies[k].wait()
        while len(outs) < len(CHUNKS) and start + CHUNKS[len(outs)] <= 32 * k + 32:
            size = CHUNKS[len(outs)]
            outs.append(
                pltpu.make_async_copy(
                    held.at[start : start + size], pieces[len(outs)], sem_out.at[len(outs)]
                )
            )
            outs[-1].start()
            start += size
        sums = lax.fori_loop(32 * k, 32 * k + (32 if k < 3 else 31), add_tap, sums, unroll=True)
    rows[0:16, :] = sums[0]
    rows[16:32, :] = sums[1]
    columns = rows[...].T
    columns = columns.astype(BF)
    lane = lax.broadcasted_iota(I32, (16, 128), 1)
    start = ((lax.axis_index("y") & 1) * 2 + lax.axis_index("xl")) * 32
    tok = jnp.zeros((16, 128), I32)
    for t in range(2):
        for b in range(16):
            tok = jnp.where(lane == start + 16 * t + b, tok_ref[t, b], tok)
    first = lax.broadcasted_iota(I32, (16, 128), 0) == 0
    tok = jnp.where(first, tok >> 4, tok & 15).astype(F32).astype(BF)
    for i in range(8):
        out_ref[i, 0:64, :] = columns[64 * i : 64 * i + 64, :]
        out_ref[i, 64:80, :] = tok
    for copy in outs:
        copy.wait()


def make_sums(tokens, filters, poles, residues, state, cache):
    return pl.pallas_call(
        sums_kernel,
        grid=(1,),
        in_specs=[
            SMEM, whole(32, 128), whole(16, 512), whole(16, 512), whole(16, 16, 512), HBM,
        ],
        out_specs=[whole(8, 80, 128)] + [HBM] * len(CHUNKS) + [whole(16, 16, 512)],
        out_shape=[jax.ShapeDtypeStruct((8, 80, 128), BF)]
        + [jax.ShapeDtypeStruct((size, 16, 512), BF) for size in CHUNKS + (16,)],
        scratch_shapes=[
            pltpu.VMEM((136, 512), F32),
            pltpu.VMEM((128, 512), F32),
            pltpu.VMEM((127, 16, 512), BF),
            pltpu.SemaphoreType.DMA((4,)),
            pltpu.SemaphoreType.DMA((len(CHUNKS),)),
        ],
        compiler_params=params(),
        name="state_sums",
    )(tokens, filters, poles, residues, state, cache)


def index_kernel(c_ref, par_ref, out_ref):
    base = c_ref[0] * 64
    lane = lax.broadcasted_iota(I32, (1, 128), 1)
    fir, onward = jnp.zeros((1, 128), I32), lane
    earlier = jnp.full((1, 128), -1, I32)
    place = lambda beam, wide: (beam >> 4) * wide + (beam & 15)
    for j in range(64):
        after = par_ref[1, base + j]
        old, older = par_ref[0, base + j] - base, par_ref[0, after] - base
        source = place(after - base, 32)
        first = lane == j // 16 * 32 + j % 16
        second = lane == j // 16 * 32 + 16 + j % 16
        fir = jnp.where(first, place(old, 128), jnp.where(second, place(older, 128) + 16, fir))
        earlier = jnp.where(second, source, earlier)
        onward = jnp.where(first, source, onward)
    out_ref[0:1, :] = fir
    out_ref[1:2, :] = fir + 32
    out_ref[2:3, :] = earlier
    out_ref[3:4, :] = onward
    out_ref[4:8, :] = jnp.zeros((4, 128), I32)


def indices(where, parents):
    return pl.pallas_call(
        index_kernel,
        grid=(1,),
        in_specs=[SMEM, SMEM],
        out_specs=whole(8, 128),
        out_shape=jax.ShapeDtypeStruct((8, 128), I32),
        compiler_params=params(),
        name="indices",
    )(where, parents)


def turn_kernel(own_ref, oth_ref, out_ref):
    for k, table in enumerate((own_ref, oth_ref)):
        out_ref[k] = table[...].T


def turn(own, oth):
    return pl.pallas_call(
        turn_kernel,
        grid=(1,),
        in_specs=[whole(512, 512)] * 2,
        out_specs=whole(2, 512, 512),
        out_shape=jax.ShapeDtypeStruct((2, 512, 512), BF),
        compiler_params=params(),
        name="turn",
    )(own, oth)


def weights(block, rows):
    return [pl.BlockSpec((1, rows // 2, 512), lambda g: (block, g, 0))] * 2


def squares_rows(x_own, x_oth):
    total = jnp.sum(x_own * x_own, axis=0, keepdims=True)
    total = total + jnp.sum(x_oth * x_oth, axis=0, keepdims=True)
    high = total.astype(BF).astype(F32)
    low = total - high
    place = lax.broadcasted_iota(I32, (EXTRA, 128), 0)
    return jnp.where(place == 0, high, jnp.where(place == 1, low, 0.0)).astype(BF)


def column(gain_ref, k):
    return jnp.broadcast_to(gain_ref[k : k + 1, :], (8, 512)).T[:, 0:1]


def hand_out(acc, rows, where_ref, outs, spread):
    half = pl.program_id(0) ^ where_ref[2]
    spread[...] = acc
    for s in range(4):
        start = pl.multiple_of(((where_ref[3] + s) & 3) * rows, rows)
        outs[s][half, 0:rows, :] = spread[pl.ds(start, rows), :]
    return half


def product_in(where_ref, w_own, w_oth, scaled, squares, spread, outs):
    acc = jnp.dot(w_own[0], scaled[0], preferred_element_type=F32)
    acc = (acc + jnp.dot(w_oth[0], scaled[1], preferred_element_type=F32)).astype(BF)
    half = hand_out(acc, 384, where_ref, outs, spread)
    for out in outs:
        out[half, 384:400, :] = squares[...]


def embed_kernel(
    c_ref, got_ref, tables, g_own, g_oth, w_own, w_oth, *refs
):
    *outs, x_ref, send_ref, scaled, squares, spread = refs

    @pl.when(pl.program_id(0) == 0)
    def _():
        c = c_ref[0]
        tok = jnp.zeros((16, 128), F32)
        for q in range(4):
            tok = tok + got_ref[c * 4 + q, 64:80, :].astype(F32)
            send_ref[q] = got_ref[4 - c * 4 + q, 0:64, :]
        vocab = lax.broadcasted_iota(I32, (512, 128), 0)
        tok = (tok[0:1, :] * 16.0 + tok[1:2, :] + 0.5).astype(I32)
        onehot = (vocab == tok).astype(BF)
        halves = []
        for k, gain in enumerate((g_own, g_oth)):
            x = jnp.dot(tables[k], onehot, preferred_element_type=F32)
            x_ref[k] = x.astype(BF)
            scaled[k] = (x * column(gain, 0)).astype(BF)
            halves.append(x)
        squares[...] = squares_rows(*halves)

    product_in(c_ref, w_own, w_oth, scaled, squares, spread, outs)


IN_SCRATCH = [
    pltpu.VMEM((2, 512, 128), BF), pltpu.VMEM((EXTRA, 128), BF), pltpu.VMEM((1536, 128), BF)
]
IN_SHAPE = [jax.ShapeDtypeStruct((2, 400, 128), BF)] * 4
IN_SPECS = [whole(2, 400, 128)] * 4
COST_IN = pl.CostEstimate(flops=2 * 3072 * 1024 * 128, bytes_accessed=7 << 20, transcendentals=0)
COST_OUT = pl.CostEstimate(flops=2 * 1024 * 1024 * 128, bytes_accessed=5 << 19, transcendentals=0)


def project_embed(where, got, tables, g_own, g_oth, w_own, w_oth):
    return pl.pallas_call(
        embed_kernel,
        grid=(2,),
        in_specs=[
            SMEM, whole(8, 80, 128), whole(2, 512, 512), whole(2, 512), whole(2, 512),
            *weights(0, 3072),
        ],
        out_specs=[*IN_SPECS, whole(2, 512, 128), whole(4, 64, 128)],
        out_shape=[
            *IN_SHAPE,
            jax.ShapeDtypeStruct((2, 512, 128), BF),
            jax.ShapeDtypeStruct((4, 64, 128), BF),
        ],
        scratch_shapes=IN_SCRATCH,
        compiler_params=params(),
        cost_estimate=COST_IN,
        name="embed_project",
    )(where, got, tables, g_own, g_oth, w_own, w_oth)


def gather_rows(c, a_ref, k):
    start = pl.multiple_of((c ^ k) * 64, 64)
    return jnp.concatenate([a_ref[i, pl.ds(start, 64), :] for i in range(8)], axis=0)


def in_kernel(c_ref, a_ref, g_own, g_oth, w_own, w_oth, *refs):
    *outs, scaled, squares, spread = refs

    @pl.when(pl.program_id(0) == 0)
    def _():
        halves = []
        for k, gain in enumerate((g_own, g_oth)):
            x = gather_rows(c_ref[0], a_ref, k).astype(F32)
            scaled[k] = (x * column(gain, 1)).astype(BF)
            halves.append(x)
        squares[...] = squares_rows(*halves)

    product_in(c_ref, w_own, w_oth, scaled, squares, spread, outs)


def project_in(where, rows, g_own, g_oth, w_own, w_oth):
    return pl.pallas_call(
        in_kernel,
        grid=(2,),
        in_specs=[
            SMEM, whole(8, 128, 128), whole(2, 512), whole(2, 512), *weights(1, 3072),
        ],
        out_specs=IN_SPECS,
        out_shape=IN_SHAPE,
        scratch_shapes=IN_SCRATCH,
        compiler_params=params(),
        cost_estimate=COST_IN,
        name="norm_project",
    )(where, rows, g_own, g_oth, w_own, w_oth)


def add_up(terms):
    *near, far = terms
    total = far[...].astype(F32)
    for term in near:
        total = total + term[0].astype(F32)
    return total


def terms_specs(rows):
    return [pl.BlockSpec((1, rows, 128), lambda g: (0, 0, 0))] * 4 + [whole(rows, 128)]


def mix_kernel(block, c_ref, *refs):
    t_own, t_oth, idx_ref, gated_ref, kv_ref = refs[5:]
    c = c_ref[0]
    total = add_up(refs[:5])
    squares = total[384:385, :] + total[385:386, :]
    feats = (total[0:384, :] * lax.rsqrt(squares / D + EPSILON)).astype(BF).astype(F32)
    kind = lambda m: jnp.concatenate(
        [feats[64 * m : 64 * m + 64, :], feats[192 + 64 * m : 256 + 64 * m, :]], axis=0
    )
    kv = (kind(1) * kind(2)).astype(BF)
    square = lax.broadcasted_iota(I32, (128, 128), 0)
    earlier = (square == idx_ref[2:3, :]).astype(BF)
    onward = (square == idx_ref[3:4, :]).astype(BF)
    kv_before = jnp.dot(kv, earlier, preferred_element_type=F32)
    kv_ref[...] = jnp.dot(kv, onward, preferred_element_type=F32).T.astype(BF)
    parts, first, second = [], [], []
    for k in range(2):
        own = c == k
        acc = jnp.zeros((64, 128), F32)
        for q in range(4):
            sums = jnp.where(own, t_own[c * 4 + q, 0:64, :].astype(F32), t_oth[q].astype(F32))
            pick = (square + 128 * q == idx_ref[block : block + 1, :]).astype(BF)
            acc = acc + jnp.dot(sums.astype(BF), pick, preferred_element_type=F32)
            if q == 0:
                gain = lambda lane: sums[:, lane : lane + 1] + sums[:, lane + 8 : lane + 9]
                first.append(gain(64 + 2 * block))
                second.append(gain(65 + 2 * block))
        parts.append(acc)
    first, second = jnp.concatenate(first, axis=0), jnp.concatenate(second, axis=0)
    filtered = first * kv.astype(F32) + second * kv_before + jnp.concatenate(parts, axis=0)
    gated = (kind(0) * filtered).astype(BF)
    for i in range(8):
        gated_ref[i] = gated


def mix(block, where, received, t_own, t_oth, idx):
    return pl.pallas_call(
        lambda *refs: mix_kernel(block, *refs),
        grid=(1,),
        in_specs=[
            SMEM, *terms_specs(400), whole(8, 80, 128), whole(4, 64, 128), whole(8, 128)
        ],
        out_specs=[whole(8, 128, 128), whole(128, 128)],
        out_shape=[
            jax.ShapeDtypeStruct((8, 128, 128), BF),
            jax.ShapeDtypeStruct((128, 128), BF),
        ],
        compiler_params=params(SMALL),
        name="mix",
    )(where, *received, t_own, t_oth, idx)


def out_kernel(c_ref, a_ref, w_own, w_oth, out_ref, rows):

    @pl.when(pl.program_id(0) == 0)
    def _():
        for k in range(2):
            rows[k] = gather_rows(c_ref[0], a_ref, k)

    acc = jnp.dot(w_own[0], rows[0], preferred_element_type=F32)
    acc = (acc + jnp.dot(w_oth[0], rows[1], preferred_element_type=F32)).astype(BF)
    for k in range(4):
        out_ref[k] = acc[128 * k : 128 * k + 128, :]


def project_out(block, where, rows, w_own, w_oth):
    return pl.pallas_call(
        out_kernel,
        grid=(2,),
        in_specs=[SMEM, whole(8, 128, 128), *weights(block, 1024)],
        out_specs=pl.BlockSpec((4, 128, 128), lambda g: (g, 0, 0)),
        out_shape=jax.ShapeDtypeStruct((8, 128, 128), BF),
        scratch_shapes=[pltpu.VMEM((2, 512, 128), BF)],
        compiler_params=params(),
        cost_estimate=COST_OUT,
        name="project_out",
    )(where, rows, w_own, w_oth)


def add_blocks(r_ref):
    total = r_ref[0].astype(F32)
    for g in range(1, 8):
        total = total + r_ref[g].astype(F32)
    return total.astype(BF).astype(F32)


def residual_kernel(c_ref, r_ref, x_ref, out_ref):
    outward = add_blocks(r_ref)
    start = pl.multiple_of(c_ref[1] * 64, 64)
    before = jnp.concatenate(
        [x_ref[c_ref[0] ^ k, pl.ds(start, 64), :] for k in range(2)], axis=0
    )
    hidden = (before.astype(F32) + outward).astype(BF)
    for i in range(8):
        out_ref[i] = hidden


def residual(where, received, embedded):
    return pl.pallas_call(
        residual_kernel,
        grid=(1,),
        in_specs=[SMEM, whole(8, 128, 128), whole(2, 512, 128)],
        out_specs=whole(8, 128, 128),
        out_shape=jax.ShapeDtypeStruct((8, 128, 128), BF),
        compiler_params=params(SMALL),
        name="residual",
    )(where, received, embedded)


def last_kernel(c_ref, r_ref, h_ref, kv0_ref, kv1_ref, keep_ref, send_ref):
    outward = add_blocks(r_ref)
    hidden = (h_ref[0].astype(F32) + outward).astype(BF).astype(F32).T
    first = c_ref[0] == 0
    kv0, kv1 = kv0_ref[...].astype(F32), kv1_ref[...].astype(F32)
    pair = lambda k: jnp.concatenate(
        [hidden[:, 64 * k : 64 * k + 64], kv0[:, 64 * k : 64 * k + 64]], axis=1
    )
    low, high = pair(0), pair(1)
    keep_ref[0] = jnp.where(first, low, high).astype(BF)
    send_ref[0] = jnp.where(first, high, low).astype(BF)
    turned = pltpu.roll(kv1, 64, 1)
    keep_ref[1] = jnp.where(first, kv1, turned).astype(BF)
    send_ref[1] = jnp.where(first, turned, kv1).astype(BF)


def last(where, received, hidden, kv0, kv1):
    return pl.pallas_call(
        last_kernel,
        grid=(1,),
        in_specs=[
            SMEM, whole(8, 128, 128), pl.BlockSpec((1, 128, 128), lambda g: (0, 0, 0)),
            whole(128, 128), whole(128, 128),
        ],
        out_specs=[whole(2, 128, 128)] * 2,
        out_shape=[jax.ShapeDtypeStruct((2, 128, 128), BF)] * 2,
        compiler_params=params(SMALL),
        name="last",
    )(where, received, hidden, kv0, kv1)


def arrange_kernel(c_ref, keep_ref, got_ref, out_ref):
    first = c_ref[0] == 0
    for k in range(2):
        keep, got = keep_ref[k].astype(F32), got_ref[k].astype(F32)
        for half in range(2):
            rows = jnp.where(first == (half == 0), keep, got).astype(BF)
            for q in range(4):
                out_ref[4 * half + q, 32 * k : 32 * k + 32, :] = rows[32 * q : 32 * q + 32, :]


def arrange(where, keep, got):
    return pl.pallas_call(
        arrange_kernel,
        grid=(1,),
        in_specs=[SMEM, whole(2, 128, 128), whole(2, 128, 128)],
        out_specs=whole(8, 64, 128),
        out_shape=jax.ShapeDtypeStruct((8, 64, 128), BF),
        compiler_params=params(SMALL),
        name="arrange",
    )(where, keep, got)


def origin(where_ref, par_ref, b):
    dp = where_ref[1]
    beam = par_ref[0, par_ref[1, dp * 16 + b]]
    return beam & 15, (beam >> 4) == dp


def reorder_kernel(where_ref, par_ref, own_ref, *refs):
    pieces, (out_ref, held, ready, sems, sem_out) = refs[: len(CHUNKS)], refs[len(CHUNKS) :]
    copies = [pltpu.make_async_copy(own_ref.at[0:125], held.at[0, 0:125], sems.at[0])]
    start = 0
    for k, size in enumerate(CHUNKS):
        copies.append(
            pltpu.make_async_copy(pieces[k], held.at[1, start : start + size], sems.at[k + 1])
        )
        start += size
    for copy in copies:
        copy.start()
    held[0, 125:128] = jnp.zeros((3, 16, 512), BF)
    held[1, 125:128] = jnp.zeros((3, 16, 512), BF)
    row = lax.broadcasted_iota(I32, (128, 256), 0)
    col = lax.broadcasted_iota(I32, (128, 256), 1)
    wanted = jnp.zeros((128, 256), I32)
    for b in range(16):
        slot, here = origin(where_ref, par_ref, b)
        wanted = jnp.where((row & 15) == b, slot + jnp.where(here, 0, 16), wanted)
    same_tap = ((col >> 4) & 7) == (row >> 4)
    pick = (same_tap & ((col & 15) + (col >> 7) * 16 == wanted)).astype(BF)
    for copy in copies:
        copy.wait()
    outs = []
    for k in range(16):
        taps = slice(8 * k, 8 * k + 8)
        both = jnp.concatenate(
            [held[0, taps].reshape(128, 512), held[1, taps].reshape(128, 512)], axis=0
        )
        moved = jnp.dot(pick, both, preferred_element_type=F32).astype(BF)
        ready[taps] = moved.reshape(8, 16, 512)
        size = 8 if k < 15 else 5
        outs.append(
            pltpu.make_async_copy(
                ready.at[8 * k : 8 * k + size], out_ref.at[8 * k + 2 : 8 * k + 2 + size],
                sem_out.at[k],
            )
        )
        outs[-1].start()
    for copy in outs:
        copy.wait()


def reorder(where, parents, own, pieces):
    return pl.pallas_call(
        reorder_kernel,
        in_specs=[SMEM, SMEM, HBM] + [HBM] * len(CHUNKS),
        out_specs=HBM,
        out_shape=jax.ShapeDtypeStruct((127, 16, 512), BF),
        scratch_shapes=[
            pltpu.VMEM((2, 128, 16, 512), BF),
            pltpu.VMEM((128, 16, 512), BF),
            pltpu.SemaphoreType.DMA((len(CHUNKS) + 1,)),
            pltpu.SemaphoreType.DMA((16,)),
        ],
        compiler_params=params(),
        cost_estimate=pl.CostEstimate(flops=1 << 29, bytes_accessed=6 << 20, transcendentals=0),
        name="reorder",
    )(where, parents, own, *pieces)


def final_kernel(
    where_ref, par_ref, r_ref, poles_ref, own_ref, oth_ref, fir_ref,
    hid_ref, fir_out, state_ref, fresh, sem,
):
    wide = lambda row, lane: jnp.concatenate(
        [r_ref[i, row : row + 16, :].astype(F32)[:, lane : lane + 64] for i in range(8)], axis=1
    )
    fresh[0] = wide(16, 64).astype(BF)
    fresh[1] = wide(0, 64).astype(BF)
    copy = pltpu.make_async_copy(fresh, fir_out.at[0:2], sem)
    copy.start()
    for t in range(2):
        hid_ref[t] = wide(16 * t, 0).astype(BF)
    before, now = wide(32, 0), wide(48, 0)
    poles = poles_ref[...]
    for b in range(16):
        slot, here = origin(where_ref, par_ref, b)
        old = jnp.where(here, own_ref[slot], oth_ref[slot].astype(F32))
        state_ref[b] = poles * (poles * old + before[b : b + 1, :]) + now[b : b + 1, :]
    copy.wait()


def final(where, parents, received, poles, own, oth, fir):
    return pl.pallas_call(
        final_kernel,
        grid=(1,),
        in_specs=[
            SMEM, SMEM, whole(8, 64, 128), whole(16, 512), whole(16, 16, 512),
            whole(16, 16, 512), HBM,
        ],
        out_specs=[whole(2, 16, 512), HBM, whole(16, 16, 512)],
        out_shape=[
            jax.ShapeDtypeStruct((2, 16, 512), BF),
            jax.ShapeDtypeStruct((127, 16, 512), BF),
            jax.ShapeDtypeStruct((16, 16, 512), F32),
        ],
        scratch_shapes=[pltpu.VMEM((2, 16, 512), BF), pltpu.SemaphoreType.DMA],
        input_output_aliases={6: 1},
        compiler_params=params(SMALL),
        name="final",
    )(where, parents, received, poles, own, oth, fir)


def local(
    tokens, parents, embed_table, norm_gain, weight_in, weight_out, fir_filters, mode_poles,
    residues, fir_cache, modal_state,
):
    dp = lax.axis_index(DP).astype(I32)
    c = lax.axis_index("c").astype(I32)
    where = jnp.stack([c, dp, lax.axis_index("xh").astype(I32), lax.axis_index("z").astype(I32)])
    w_in = weight_in.reshape(2, 3072, 512)
    w_out = weight_out.reshape(2, 1024, 512)
    cache = jnp.transpose(fir_cache, (1, 0, 2))
    e_oth = swap(embed_table, "c")
    g_oth = swap(norm_gain, "c")
    sums, *pieces = make_sums(
        tokens, fir_filters, mode_poles, residues, modal_state, cache
    )
    w_in, w_out, e_oth, g_oth, sums = lax.optimization_barrier(
        (w_in, w_out, e_oth, g_oth, sums)
    )
    w_in_oth = swap(w_in, "c")
    w_out_oth = swap(w_out, "c")
    moved = []

    def send(trigger):
        piece, trigger, moved[-1:] = lax.optimization_barrier(
            (pieces[len(moved)], trigger, moved[-1:])
        )
        moved.append(swap(piece, "xl"))
        return trigger

    def scatter(terms):
        terms = list(terms)
        for s in (2, 1, 3):
            terms[s] = lax.ppermute(terms[s], "z", [(z, (z + s) % 4) for z in range(4)])
        far = sum(term[1].astype(F32) for term in terms).astype(BF)
        far, moved[-1] = lax.optimization_barrier((far, moved[-1]))
        return *terms, swap(far, "xh")

    idx = indices(where, parents)
    tables = turn(embed_table, e_oth)
    got, idx, tables = lax.optimization_barrier((exchange(sums, DP), idx, tables))
    *partial, embedded, t_send = project_embed(
        where, send(got), tables, norm_gain, g_oth, w_in, w_in_oth
    )
    t_oth = swap(t_send, "c")
    def gather(rows):
        rows, moved[-1] = lax.optimization_barrier((exchange(send(rows), DP), moved[-1]))
        return rows

    gated, kv0 = mix(0, where, scatter(partial), got, t_oth, idx)
    partial = project_out(0, where, gather(gated), w_out, w_out_oth)
    hidden = residual(where, exchange(partial, XZ), embedded)
    rows = send(exchange(hidden, DP))
    partial = project_in(where, rows, norm_gain, g_oth, w_in, w_in_oth)
    gated, kv1 = mix(1, where, scatter(partial), got, t_oth, idx)
    partial = project_out(1, where, gather(gated), w_out, w_out_oth)
    keep, crossing = last(where, exchange(partial, XZ), hidden, kv0, kv1)
    received = exchange(arrange(where, keep, swap(crossing, "c")), DP)
    *moved, state_oth = moved
    fir_before = reorder(where, parents, cache, moved)
    hidden_out, fir_next, state_next = final(
        where, parents, received, mode_poles, modal_state, state_oth, fir_before
    )
    return hidden_out, jnp.transpose(fir_next, (1, 0, 2)), state_next


def solution(mesh):
    fine = Mesh(mesh.devices.reshape(4, 2, 2, 4, 2), ("y", "xl", "xh", "z", "c"))
    return jax.shard_map(
        local,
        mesh=fine,
        in_specs=(
            P(None, DP),
            P(),
            P(None, CHAN),
            P(None, CHAN),
            P(None, None, DP, None, None, CHAN),
            P(None, None, DP, None, CHAN),
            P(CHAN, None),
            P(None, CHAN),
            P(None, CHAN),
            P(DP, None, CHAN),
            P(DP, None, CHAN),
        ),
        out_specs=(P(None, DP, CHAN), P(DP, None, CHAN), P(DP, None, CHAN)),
        check_vma=False,
    )
```
